128 devices in a mesh: dp: 8 (over x, core), ctx: 16 (over y, z).
Axes of the slice: x: 4, y: 4, z: 4, core: 2. Of those that a mesh axis runs over, the one named last changes fastest.
Arguments:
- inputs: bfloat16 [16384, 960], P(('dp', 'ctx')), may hold values from -6 to 6
- positions: int32 [16384], P(('dp', 'ctx')), may hold values from 0 to 2047, as said below
- attn_gain: bfloat16 [960], P('dp'), may hold values from 0.099609375 to 1.8984375
- w_query: bfloat16 [960, 960], P('dp'), may hold values from -0.1875 to 0.1875
- w_key: bfloat16 [960, 320], P('dp'), may hold values from -0.1875 to 0.1875
- w_value: bfloat16 [960, 320], P('dp'), may hold values from -0.1875 to 0.1875
- w_out: bfloat16 [960, 960], P('dp'), may hold values from -0.75 to 0.75
- mlp_gain: bfloat16 [960], P('dp'), may hold values from 0.099609375 to 1.8984375
- w_gate: bfloat16 [960, 2560], P('dp'), may hold values from -0.1875 to 0.1875
- w_up: bfloat16 [960, 2560], P('dp'), may hold values from -0.1875 to 0.1875
- w_down: bfloat16 [2560, 960], P('dp'), may hold values from -0.125 to 0.125
- cotangent: bfloat16 [16384, 960], P(('dp', 'ctx')), may hold values from -6 to 6
Outputs:
- output: bfloat16 [16384, 960], P(('dp', 'ctx'))
- input_grad: float32 [16384, 960], P(('dp', 'ctx'))
- attn_gain_grad: float32 [960], P('dp')
- query_grad: float32 [960, 960], P('dp')
- key_grad: float32 [960, 320], P('dp')
- value_grad: float32 [960, 320], P('dp')
- out_grad: float32 [960, 960], P('dp')
- mlp_gain_grad: float32 [960], P('dp')
- gate_grad: float32 [960, 2560], P('dp')
- up_grad: float32 [960, 2560], P('dp')
- down_grad: float32 [2560, 960], P('dp')
The draws below stay inside these ranges and needn't reach their ends.
Inputs may be any that keep to these rules, and one draw needn't show every extreme that they name: Within each sequence of 2048 tokens the positions come in blocks of 128 consecutive values, one block on each device of ctx, in an order drawn from the seed; together they take each value 0 to 2047 once.
All inputs are finite; a program needn't handle non-finite values.
Results may differ from the reference program's by a relative error of at most 0.03.
Values may be sent and summed in bfloat16 or wider, within the bound.
No kernel may reach another device: no remote copies, remote signals or barrier semaphores. Data moves between devices by JAX's collectives and lax.ppermute only.
A program may use at most 128 MiB of HBM per device.

```python
import jax
import jax.numpy as jnp
from jax import lax

D = 960
HEADS = 15
KV_HEADS = 5
HEAD_DIM = 64
FF = 2560
TOK_DEV = 128
LENGTH = 2048
SEQS = 8
TOKENS = 16384
Q_WIDTH = 960
KV_WIDTH = 320


def draw_positions(key, part):
    key = jax.random.fold_in(key, 11)
    blocks = LENGTH // TOK_DEV
    orders = jax.vmap(lambda single: jax.random.permutation(single, blocks))(jax.random.split(key, SEQS))
    places = orders[:, :, None] * TOK_DEV + jnp.arange(TOK_DEV)[None, None, :]
    return places.reshape(TOKENS).astype(jnp.int32)


def shard_levels(stream_key, dims, pieces, least, largest):
    def one(dim, parts):
        steps = jax.random.uniform(jax.random.fold_in(jax.random.fold_in(stream_key, 6), dim), (parts,), jnp.float32, least / len(pieces), largest / len(pieces))
        return jnp.repeat(jnp.exp(steps), dims[dim] // parts).reshape((-1,) + (1,) * (len(dims) - dim - 1))

    factor_of = one(*pieces[0])
    for cut in pieces[1:]:
        factor_of = factor_of * one(*cut)
    return factor_of


def gaussian(stream_key, dims, deviation, limit, pieces=(), dtype=jnp.bfloat16):
    drawn = deviation * jax.random.normal(stream_key, dims, jnp.float32)
    if pieces:
        drawn = drawn * shard_levels(stream_key, dims, pieces, -0.22, 0.18)
    return jnp.clip(drawn, -limit, limit).astype(dtype)


def setup_inputs(seed: int = 0) -> dict:
    seeds = jax.random.split(jax.random.key(seed), 13)
    return {
        "inputs": gaussian(seeds[0], (TOKENS, D), 1.0, 6.0, ((0, 128),)),
        "positions": draw_positions(jax.random.fold_in(seeds[12], 71), 0),
        "attn_gain": jnp.clip(1.0 + 0.18 * jax.random.normal(seeds[2], (D,), jnp.float32), 0.099609375, 1.8984375).astype(jnp.bfloat16),
        "w_query": gaussian(seeds[3], (D, Q_WIDTH), D ** -0.5, 0.1875, ((0, 8),)),
        "w_key": gaussian(seeds[4], (D, KV_WIDTH), D ** -0.5, 0.1875, ((0, 8),)),
        "w_value": gaussian(seeds[5], (D, KV_WIDTH), D ** -0.5, 0.1875, ((0, 8),)),
        "w_out": gaussian(seeds[6], (Q_WIDTH, D), (Q_WIDTH // 16) ** -0.5, 0.75, ((0, 8),)),
        "mlp_gain": jnp.clip(1.0 + 0.18 * jax.random.normal(seeds[7], (D,), jnp.float32), 0.099609375, 1.8984375).astype(jnp.bfloat16),
        "w_gate": gaussian(seeds[8], (D, FF), D ** -0.5, 0.1875, ((0, 8),)),
        "w_up": gaussian(seeds[9], (D, FF), D ** -0.5, 0.1875, ((0, 8),)),
        "w_down": gaussian(seeds[10], (FF, D), FF ** -0.5, 0.125, ((0, 8),)),
        "cotangent": gaussian(seeds[11], (TOKENS, D), 1.0, 6.0, ((0, 128),)),
    }


rope_base = 100000.0
norm_eps = 1e-05
highest = lax.Precision.HIGHEST

@jax.custom_vjp
def low(v):
    return lax.optimization_barrier(v.astype(jnp.bfloat16)).astype(jnp.float32)

@jax.custom_vjp
def low_back(v):
    return v

def low_keep(v):
    return (low(v), None)

def low_pass(kept, grad):
    return (grad,)

def back_keep(v):
    return (v, None)

def back_low(kept, grad):
    return (low(grad),)
low.defvjp(low_keep, low_pass)
low_back.defvjp(back_keep, back_low)

def rope(values, places):
    half = HEAD_DIM // 2
    freq = rope_base ** (-2.0 * jnp.arange(half).astype(jnp.float32) / HEAD_DIM)
    turn = places.astype(jnp.float32)[..., None] * freq
    angle_cos = jnp.cos(turn)[..., None, :]
    angle_sin = jnp.sin(turn)[..., None, :]
    first = values[..., :half]
    second = values[..., half:]
    return jnp.concatenate([first * angle_cos - second * angle_sin, second * angle_cos + first * angle_sin], -1)

def rms_norm(values, gain):
    return values * lax.rsqrt(lax.optimization_barrier(jnp.mean(values * values, axis=-1, keepdims=True)) + norm_eps) * gain

def matmul(left, right):
    return jnp.dot(left, right, precision=highest)

def seq_attention(args):
    query, keys, values, places = args
    block = min(512, LENGTH)
    count = LENGTH // block
    group = HEADS // KV_HEADS
    query_blocks = query.reshape(count, block, KV_HEADS, group, HEAD_DIM)
    place_blocks = places.reshape(count, block)

    def one_block(pair):
        rows, row_places = pair
        scores = jnp.einsum('tgrd,sgd->tgrs', rows, keys, precision=highest) * HEAD_DIM ** (-0.5)
        scores = low_back(scores)
        visible = places[None, None, None, :] <= row_places[:, None, None, None]
        scores = jnp.where(visible, scores, -1e+30)
        top = lax.optimization_barrier(jnp.max(scores, axis=-1, keepdims=True))
        weights = jnp.exp(scores - top)
        weights = weights / lax.optimization_barrier(jnp.sum(weights, axis=-1, keepdims=True))
        weights = low(weights)
        return jnp.einsum('tgrs,sgd->tgrd', weights, values, precision=highest)
    result = lax.map(jax.checkpoint(one_block), (query_blocks, place_blocks))
    return result.reshape(LENGTH, HEADS * HEAD_DIM)

def reference(inputs, positions, attn_gain, w_query, w_key, w_value, w_out, mlp_gain, w_gate, w_up, w_down, cotangent):
    places = positions.reshape(SEQS, LENGTH)

    def forward(resid, gain_one, query_w, key_w, value_w, out_w, gain_two, gate_w, up_w, down_w):
        hidden = low(rms_norm(resid, gain_one))
        query = low_back(matmul(hidden, query_w)).reshape(SEQS, LENGTH, HEADS, HEAD_DIM)
        keys = low_back(matmul(hidden, key_w)).reshape(SEQS, LENGTH, KV_HEADS, HEAD_DIM)
        values = low(low_back(matmul(hidden, value_w))).reshape(SEQS, LENGTH, KV_HEADS, HEAD_DIM)
        query = low(rope(query, places))
        keys = low(rope(keys, places))
        attn = lax.map(seq_attention, (query, keys, values, places))
        attn = low(low_back(attn.reshape(TOKENS, HEADS * HEAD_DIM)))
        mixed = resid + low_back(matmul(attn, out_w))
        hidden_two = low(rms_norm(mixed, gain_two))
        gate = low_back(matmul(hidden_two, gate_w))
        upper = low_back(matmul(hidden_two, up_w))
        middle = low(jax.nn.silu(gate) * upper)
        return mixed + matmul(middle, down_w)
    prims = tuple((a.astype(jnp.float32) for a in (inputs, attn_gain, w_query, w_key, w_value, w_out, mlp_gain, w_gate, w_up, w_down)))
    result, pullback = jax.vjp(forward, *prims)
    grads = pullback(cotangent.astype(jnp.float32))
    return (result.astype(jnp.bfloat16), grads[0], grads[1], grads[2], grads[3], grads[4], grads[5], grads[6], grads[7], grads[8], grads[9])
```

```python
import jax
import jax.numpy as jnp
from jax import lax
from jax.experimental import pallas as pl
from jax.experimental.pallas import tpu as pltpu
from jax.sharding import Mesh
from jax.sharding import PartitionSpec as P

HEADS = 15
KV_HEADS = 5
GROUP = HEADS // KV_HEADS
HEAD_DIM = 64
HALF = HEAD_DIM // 2
Q_WIDTH = HEADS * HEAD_DIM
KV_WIDTH = KV_HEADS * HEAD_DIM
QKV = Q_WIDTH + 2 * KV_WIDTH
SCALE = HEAD_DIM**-0.5
ROPE_BASE = 100000.0
NORM_EPS = 1e-05
BLOCK = 128
BLOCKS = 16
PAIR = 2 * BLOCK
LENGTH = BLOCK * BLOCKS

DP = ("x", "core")
CTX = ("ctx_0", "ctx_1")
ALL = DP + CTX

f32 = jnp.float32
bf16 = jnp.bfloat16
VMEM_LIMIT = 56 * 1024 * 1024


def exchange(chunks, axis):
    return lax.all_to_all(chunks, axis, split_axis=0, concat_axis=0, tiled=True)


def spread(shard, axis):
    return exchange(jnp.broadcast_to(shard, (lax.axis_size(axis), *shard.shape)), axis)


def other_core(value):
    return lax.ppermute(value, "core", [(0, 1), (1, 0)])


def core_order(own, other, axis):
    first = lax.axis_index("core") == 0
    return jnp.where(
        first,
        jnp.concatenate([own, other], axis),
        jnp.concatenate([other, own], axis),
    )


def core_halves(value, axis):
    core = lax.axis_index("core")
    keep = lax.dynamic_index_in_dim(value, core, axis, keepdims=False)
    give = lax.dynamic_index_in_dim(value, 1 - core, axis, keepdims=False)
    return keep, give


def core_summed(value, axis):
    keep, give = core_halves(value, axis)
    return (keep + other_core(give.astype(bf16)).astype(f32)).astype(bf16)


def total(parts):
    return jnp.sum(parts.astype(f32), axis=0)


def dot(left, right, left_dim, right_dim):
    return lax.dot_general(
        left, right, (((left_dim,), (right_dim,)), ((), ())), preferred_element_type=f32
    )


def rotate_rows(first, second, cos, sin):
    return first * cos - second * sin, second * cos + first * sin


def norm_back(normed, root, gain, grad_normed, grad_out):
    weighted = gain * grad_normed
    return (
        grad_out
        + root * weighted
        - normed * root * jnp.mean(normed * weighted, axis=-1, keepdims=True)
    )


def flip(block):
    return block.astype(f32).T.astype(bf16)


def scores_of(keys, query, key_places, query_places, span):
    scores = jnp.dot(keys, query, preferred_element_type=f32)
    places = key_places[span - 512 : span, :]
    visible = jnp.concatenate([places, places], 1) <= query_places
    tail = jnp.where(visible, scores[span - 512 :], -1e30)
    if span == 512:
        return tail
    return jnp.concatenate([scores[: span - 512], tail], 0)


def sort_places(block, rank, places, key_places, query_places):
    row = places[block]
    query_places[rank // 2, :, (rank % 2) * BLOCK : (rank % 2 + 1) * BLOCK] = row
    key_places[rank * BLOCK : (rank + 1) * BLOCK, :] = jnp.broadcast_to(row, (BLOCK, BLOCK)).T


def forward_kernel(
    order, qkv, places, attn, attn_full, log_total, keys, values, query, key_places, query_places
):
    for rank in range(BLOCKS):
        block = order[rank]
        rows = slice(rank * BLOCK, (rank + 1) * BLOCK)
        side = slice((rank % 2) * BLOCK, (rank % 2 + 1) * BLOCK)
        query[rank // 2, :, side] = qkv[block, 0:64, :]
        keys[rows, :] = flip(qkv[block, 64:128, :])
        values[:, rows] = qkv[block, 128:192, :]
        sort_places(block, rank, places, key_places, query_places)
    for quarter in range(4):
        span = 512 * (quarter + 1)

        def pair_step(step, carry, quarter=quarter, span=span):
            pair = 2 * quarter + step
            scores = scores_of(keys[:span, :], query[pair], key_places, query_places[pair], span)
            best = jnp.max(scores, axis=0, keepdims=True)
            weights = jnp.exp(scores - best)
            sums = jnp.sum(weights, axis=0, keepdims=True)
            result = jnp.dot(values[:, :span], weights.astype(bf16), preferred_element_type=f32)
            result = result / sums
            attn_full[pair] = result
            log_total[pair] = best + jnp.log(sums)
            low = result.astype(bf16)
            attn[order[2 * pair]] = low[:, :BLOCK]
            attn[order[2 * pair + 1]] = low[:, BLOCK:]
            return carry

        lax.fori_loop(0, 2, pair_step, 0)


def backward_kernel(
    order,
    qkv,
    places,
    grad_attn,
    attn_full,
    log_total,
    cos,
    sin,
    grad,
    keys,
    keys_wide,
    values,
    query,
    query_tall,
    out_wide,
    out_tall,
    key_places,
    query_places,
    grad_keys,
    grad_values,
):
    for rank in range(BLOCKS):
        block = order[rank]
        rows = slice(rank * BLOCK, (rank + 1) * BLOCK)
        side = slice((rank % 2) * BLOCK, (rank % 2 + 1) * BLOCK)
        query[rank // 2, :, side] = qkv[block, 0:64, :]
        query_tall[rank // 2, side, :] = flip(qkv[block, 0:64, :])
        keys_wide[:, rows] = qkv[block, 64:128, :]
        keys[rows, :] = flip(qkv[block, 64:128, :])
        values[rows, :] = flip(qkv[block, 128:192, :])
        out_wide[rank // 2, :, side] = grad_attn[block]
        out_tall[rank // 2, side, :] = flip(grad_attn[block])
        sort_places(block, rank, places, key_places, query_places)
    grad_keys[...] = jnp.zeros_like(grad_keys)
    grad_values[...] = jnp.zeros_like(grad_values)
    for quarter in range(4):
        span = 512 * (quarter + 1)

        def pair_step(step, carry, quarter=quarter, span=span):
            pair = 2 * quarter + step
            scores = scores_of(keys[:span, :], query[pair], key_places, query_places[pair], span)
            probs = jnp.exp(scores - log_total[pair])
            grad_probs = jnp.dot(values[:span, :], out_wide[pair], preferred_element_type=f32)
            delta = jnp.sum(out_wide[pair].astype(f32) * attn_full[pair], axis=0, keepdims=True)
            grad_scores = (probs * (grad_probs - delta)).astype(bf16)
            grad_query = SCALE * jnp.dot(
                keys_wide[:, :span], grad_scores, preferred_element_type=f32
            )
            grad_keys[:span, :] += jnp.dot(
                grad_scores, query_tall[pair], preferred_element_type=f32
            )
            grad_values[:span, :] += jnp.dot(
                probs.astype(bf16), out_tall[pair], preferred_element_type=f32
            )
            for part in range(2):
                block = order[2 * pair + part]
                piece = grad_query[:, part * BLOCK : (part + 1) * BLOCK]
                first, second = rotate_rows(piece[:HALF], piece[HALF:], cos[block], -sin[block])
                grad[block, 0:32, :] = first.astype(bf16)
                grad[block, 32:64, :] = second.astype(bf16)
            return carry

        lax.fori_loop(0, 2, pair_step, 0)
    for rank in range(BLOCKS):
        block = order[rank]
        rows = slice(rank * BLOCK, (rank + 1) * BLOCK)
        piece = grad_keys[rows, :].T
        first, second = rotate_rows(piece[:HALF], piece[HALF:], cos[block], -sin[block])
        grad[block, 64:96, :] = first.astype(bf16)
        grad[block, 96:128, :] = second.astype(bf16)
        grad[block, 128:192, :] = grad_values[rows, :].T.astype(bf16)


def whole(count):
    return [pl.BlockSpec(memory_space=pltpu.SMEM)] + [pl.BlockSpec(memory_space=pltpu.VMEM)] * count


def attend(order, qkv, places):
    vmem = pl.BlockSpec(memory_space=pltpu.VMEM)
    return pl.pallas_call(
        forward_kernel,
        out_shape=(
            jax.ShapeDtypeStruct((BLOCKS, HEAD_DIM, BLOCK), bf16),
            jax.ShapeDtypeStruct((BLOCKS // 2, HEAD_DIM, PAIR), f32),
            jax.ShapeDtypeStruct((BLOCKS // 2, 1, PAIR), f32),
        ),
        in_specs=whole(2),
        out_specs=(vmem, vmem, vmem),
        scratch_shapes=[
            pltpu.VMEM((LENGTH, HEAD_DIM), bf16),
            pltpu.VMEM((HEAD_DIM, LENGTH), bf16),
            pltpu.VMEM((BLOCKS // 2, HEAD_DIM, PAIR), bf16),
            pltpu.VMEM((LENGTH, BLOCK), f32),
            pltpu.VMEM((BLOCKS // 2, 1, PAIR), f32),
        ],
        compiler_params=pltpu.CompilerParams(vmem_limit_bytes=VMEM_LIMIT),
        name="attend",
    )(order, qkv, places)


def attend_back(order, qkv, places, grad_attn, attn_full, log_total, cos, sin):
    return pl.pallas_call(
        backward_kernel,
        out_shape=jax.ShapeDtypeStruct((BLOCKS, 3 * HEAD_DIM, BLOCK), bf16),
        in_specs=whole(7),
        out_specs=pl.BlockSpec(memory_space=pltpu.VMEM),
        scratch_shapes=[
            pltpu.VMEM((LENGTH, HEAD_DIM), bf16),
            pltpu.VMEM((HEAD_DIM, LENGTH), bf16),
            pltpu.VMEM((LENGTH, HEAD_DIM), bf16),
            pltpu.VMEM((BLOCKS // 2, HEAD_DIM, PAIR), bf16),
            pltpu.VMEM((BLOCKS // 2, PAIR, HEAD_DIM), bf16),
            pltpu.VMEM((BLOCKS // 2, HEAD_DIM, PAIR), bf16),
            pltpu.VMEM((BLOCKS // 2, PAIR, HEAD_DIM), bf16),
            pltpu.VMEM((LENGTH, BLOCK), f32),
            pltpu.VMEM((BLOCKS // 2, 1, PAIR), f32),
            pltpu.VMEM((LENGTH, HEAD_DIM), f32),
            pltpu.VMEM((LENGTH, HEAD_DIM), f32),
        ],
        compiler_params=pltpu.CompilerParams(vmem_limit_bytes=VMEM_LIMIT),
        name="attend_back",
    )(order, qkv, places, grad_attn, attn_full, log_total, cos, sin)


def body(
    inputs,
    positions,
    attn_gain,
    w_query,
    w_key,
    w_value,
    w_out,
    mlp_gain,
    w_gate,
    w_up,
    w_down,
    cotangent,
):
    rows, width = inputs.shape
    shard = w_query.shape[0]
    hidden = w_gate.shape[1] // lax.axis_size("x")
    chips = lax.axis_size("x")

    packed = jnp.concatenate(
        [
            w_query,
            w_key,
            w_value,
            attn_gain[:, None],
            mlp_gain[:, None],
            jnp.zeros((shard, 62), bf16),
        ],
        1,
    )
    packed = lax.all_gather(packed, DP, axis=0, tiled=True)
    qkv_w = packed[:, :QKV]
    gains = packed[:, QKV : QKV + 2].astype(f32).T
    gain_one, gain_two = gains[0:1], gains[1:2]
    all_places = spread(positions[None, :], CTX)
    rank = all_places[:, 0, 0] // BLOCK
    order = jnp.sum(
        jnp.where(
            rank[None, :] == jnp.arange(BLOCKS)[:, None], jnp.arange(BLOCKS)[None, :], 0
        ),
        axis=1,
    ).astype(jnp.int32)
    freq = ROPE_BASE ** (-2.0 * jnp.arange(HALF).astype(f32) / HEAD_DIM)
    places = all_places.astype(f32)
    turns = places * freq[None, :, None]
    cos_all, sin_all = jnp.cos(turns), jnp.sin(turns)
    turn = positions.astype(f32)[None, :] * freq[:, None]
    cos, sin = jnp.cos(turn), jnp.sin(turn)

    resid = inputs.astype(f32)
    root_one = lax.rsqrt(jnp.mean(resid * resid, axis=-1, keepdims=True) + NORM_EPS)
    normed_one = resid * root_one
    hidden_one = (normed_one * gain_one).astype(bf16)

    lin = dot(qkv_w, hidden_one, 0, 1)

    def rotated(part, heads):
        part = part.reshape(heads, 2, HALF, rows)
        first, second = rotate_rows(part[:, 0], part[:, 1], cos, sin)
        return jnp.concatenate([first, second], 1)

    query = (rotated(lin[:Q_WIDTH], HEADS).astype(bf16).astype(f32) * SCALE).astype(bf16)
    keys = rotated(lin[Q_WIDTH : Q_WIDTH + KV_WIDTH], KV_HEADS).astype(bf16)
    values = lin[Q_WIDTH + KV_WIDTH :].astype(bf16).reshape(KV_HEADS, HEAD_DIM, rows)
    chunks = jnp.concatenate(
        [query, jnp.repeat(keys, GROUP, axis=0), jnp.repeat(values, GROUP, axis=0)], 1
    )
    chunks = jnp.concatenate([chunks, jnp.zeros((1, 3 * HEAD_DIM, rows), bf16)], 0)
    qkv = exchange(chunks, CTX)

    out_w = lax.all_gather(w_out, DP, axis=0, tiled=True)
    gate_up = jnp.concatenate(
        [
            jnp.swapaxes(w_gate.reshape(shard, chips, hidden), 0, 1),
            jnp.swapaxes(w_up.reshape(shard, chips, hidden), 0, 1),
        ],
        2,
    )
    gate_up = exchange(gate_up, "x")
    gate_up = core_order(gate_up[:, None], other_core(gate_up)[:, None], 1)
    gate_up = gate_up.reshape(width, 2 * hidden)
    down_w = core_order(w_down, other_core(w_down), 0)
    dy = spread(cotangent, "x").reshape(chips * rows, width)

    attn, attn_full, log_total = attend(order, qkv, places)
    attn_t = exchange(attn, CTX)[:HEADS].reshape(Q_WIDTH, rows)

    mixed = resid + dot(attn_t, out_w, 0, 0)
    root_two = lax.rsqrt(jnp.mean(mixed * mixed, axis=-1, keepdims=True) + NORM_EPS)
    normed_two = mixed * root_two
    hidden_two = (normed_two * gain_two).astype(bf16)
    hidden_two = spread(hidden_two, "x").reshape(chips * rows, width)

    early, _ = lax.optimization_barrier((hidden_one, attn_t))
    seq_hidden = spread(early, CTX)

    both = dot(hidden_two, gate_up, 1, 0)
    gate, upper = both[:, :hidden], both[:, hidden:]
    sigma = jax.nn.sigmoid(gate)
    silu_gate = gate * sigma
    middle = (silu_gate * upper).astype(bf16)
    grad_middle = dot(dy, down_w, 1, 1)
    grad_both = jnp.concatenate(
        [
            (grad_middle * upper * sigma * (1.0 + gate * (1.0 - sigma))).astype(bf16),
            (grad_middle * silu_gate).astype(bf16),
        ],
        1,
    )
    grad_hidden = dot(grad_both, gate_up, 1, 1).astype(bf16).reshape(chips, rows, width)
    grad_hidden = total(exchange(grad_hidden, "x"))
    out_part = dot(middle, down_w, 1, 0).astype(bf16).reshape(chips, rows, width)
    output = (mixed + total(exchange(out_part, "x"))).astype(bf16)

    grad_down = dot(middle, dy, 0, 0)
    grad_gate_up = dot(hidden_two, grad_both, 0, 0)

    grad_mixed = norm_back(normed_two, root_two, gain_two, grad_hidden, cotangent.astype(f32))
    grad_proj = grad_mixed.astype(bf16)
    grad_attn = dot(out_w, grad_proj, 1, 1).astype(bf16).reshape(HEADS, HEAD_DIM, rows)
    grad_attn = jnp.concatenate([grad_attn, jnp.zeros((1, HEAD_DIM, rows), bf16)], 0)
    grad_attn = exchange(grad_attn, CTX)
    grad_out = dot(attn_t, grad_proj, 1, 0)

    gd = core_summed(grad_down.reshape(2, hidden // 2, width), 0)
    gd = total(exchange(gd.reshape(BLOCKS, hidden // 2 // BLOCKS, width), CTX)).astype(bf16)
    down_grad = spread(gd, CTX).reshape(hidden // 2, width).astype(f32)

    go = core_summed(grad_out.reshape(chips, 2, shard, width), 1)
    gg = core_summed(grad_gate_up.reshape(chips, 2, shard, 2 * hidden), 1)
    go = total(exchange(go, "x")).astype(bf16)
    pieces = BLOCKS
    tall = 8 * pieces

    def by_pieces(value):
        lead = value.shape[:-2]
        pad = [(0, 0)] * len(lead) + [(0, tall - shard), (0, 0)]
        value = jnp.pad(value, pad).reshape(*lead, pieces, 8, value.shape[-1])
        return jnp.moveaxis(value, len(lead), 0)

    go = total(exchange(by_pieces(go), CTX)).astype(bf16)
    gg = total(exchange(by_pieces(gg), CTX)).astype(bf16)
    gg = exchange(gg, "x")
    gg = jnp.concatenate([gg[k] for k in range(chips)] + [go], 1)
    gg = spread(gg, CTX).reshape(tall, -1)[:shard].astype(f32)
    out_grad = gg[:, 2 * hidden * chips :]
    gg = gg[:, : 2 * hidden * chips].reshape(shard, chips, 2, hidden)
    gate_grad = gg[:, :, 0].reshape(shard, chips * hidden)
    up_grad = gg[:, :, 1].reshape(shard, chips * hidden)

    grad = attend_back(order, qkv, places, grad_attn, attn_full, log_total, cos_all, sin_all)
    back = exchange(grad, CTX)
    proj_grad = lax.dot_general(
        seq_hidden, grad, (((0, 1), (0, 2)), ((), ())), preferred_element_type=f32
    )
    proj_grad = proj_grad.astype(bf16).reshape(2 * chips, shard, 3 * HEAD_DIM)
    proj_grad = total(exchange(proj_grad, DP)).astype(bf16)
    proj_grad = spread(proj_grad, CTX)[:HEADS].astype(f32)

    def side_by_side(value):
        return jnp.swapaxes(value, 0, 1).reshape(shard, -1)

    query_grad = side_by_side(proj_grad[:, :, :HEAD_DIM])
    grouped = proj_grad.reshape(KV_HEADS, GROUP, shard, 3 * HEAD_DIM)
    kv_grad = grouped[:, 0] + grouped[:, 1] + grouped[:, 2]
    key_grad = side_by_side(kv_grad[:, :, HEAD_DIM : 2 * HEAD_DIM])
    value_grad = side_by_side(kv_grad[:, :, 2 * HEAD_DIM :])

    back = back[:HEADS]
    grad_kv = total(jnp.moveaxis(back[:, HEAD_DIM:].reshape(KV_HEADS, GROUP, 2 * HEAD_DIM, rows), 1, 0))
    grad_kv = grad_kv.astype(bf16)
    grad_lin = jnp.concatenate(
        [
            back[:, :HEAD_DIM].reshape(Q_WIDTH, rows),
            grad_kv[:, :HEAD_DIM].reshape(KV_WIDTH, rows),
            grad_kv[:, HEAD_DIM:].reshape(KV_WIDTH, rows),
        ],
        0,
    )
    grad_hidden_one = dot(grad_lin, qkv_w, 0, 1)
    input_grad = norm_back(normed_one, root_one, gain_one, grad_hidden_one, grad_mixed)

    attn_gain_grad = (
        jnp.sum(w_query.astype(f32) * query_grad, axis=1)
        + jnp.sum(w_key.astype(f32) * key_grad, axis=1)
        + jnp.sum(w_value.astype(f32) * value_grad, axis=1)
    ) / attn_gain.astype(f32)
    mlp_gain_grad = (
        jnp.sum(w_gate.astype(f32) * gate_grad, axis=1)
        + jnp.sum(w_up.astype(f32) * up_grad, axis=1)
    ) / mlp_gain.astype(f32)
    return (
        output,
        input_grad,
        attn_gain_grad,
        query_grad,
        key_grad,
        value_grad,
        out_grad,
        mlp_gain_grad,
        gate_grad,
        up_grad,
        down_grad,
    )


def solution(mesh):
    torus = Mesh(mesh.devices.reshape(4, 2, 4, 4), ALL)
    placed = (
        P(ALL, None),
        P(ALL),
        P(DP),
        P(DP, None),
        P(DP, None),
        P(DP, None),
        P(DP, None),
        P(DP),
        P(DP, None),
        P(DP, None),
        P(DP, None),
        P(ALL, None),
    )
    return jax.shard_map(
        body,
        mesh=torus,
        in_specs=placed,
        out_specs=(
            P(ALL, None),
            P(ALL, None),
            P(DP),
            P(DP, None),
            P(DP, None),
            P(DP, None),
            P(DP, None),
            P(DP),
            P(DP, None),
            P(DP, None),
            P(DP, None),
        ),
        check_vma=False,
    )
```

```python
import jax
import jax.numpy as jnp
from jax import lax
from jax.experimental import pallas as pl
from jax.experimental.pallas import tpu as pltpu
from jax.sharding import Mesh
from jax.sharding import PartitionSpec as P

HEADS = 15
KV_HEADS = 5
GROUP = HEADS // KV_HEADS
HEAD_DIM = 64
HALF = HEAD_DIM // 2
Q_WIDTH = HEADS * HEAD_DIM
KV_WIDTH = KV_HEADS * HEAD_DIM
QKV = Q_WIDTH + 2 * KV_WIDTH
SCALE = HEAD_DIM**-0.5
ROPE_BASE = 100000.0
NORM_EPS = 1e-05
BLOCK = 128
BLOCKS = 16
PAIR = 2 * BLOCK
LENGTH = BLOCK * BLOCKS

DP = ("x", "core")
CTX = ("ctx_0", "ctx_1")
ALL = DP + CTX

f32 = jnp.float32
bf16 = jnp.bfloat16
VMEM_LIMIT = 56 * 1024 * 1024


def exchange(chunks, axis):
    return lax.all_to_all(chunks, axis, split_axis=0, concat_axis=0, tiled=True)


def spread(shard, axis):
    return exchange(jnp.broadcast_to(shard, (lax.axis_size(axis), *shard.shape)), axis)


def other_core(value):
    return lax.ppermute(value, "core", [(0, 1), (1, 0)])


def shift(value, steps):
    return lax.ppermute(value, "x", [(k, (k + steps) % 4) for k in range(4)])


def from_chips(value):
    return [value, shift(value, 1), shift(value, 3), shift(value, 2)]


def to_chips(parts):
    sent = [shift(parts[1], 3), shift(parts[2], 1), shift(parts[3], 2)]
    return parts[0].astype(f32) + sent[0].astype(f32) + sent[1].astype(f32) + sent[2].astype(f32)


def core_order(own, other, axis):
    first = lax.axis_index("core") == 0
    return jnp.where(
        first,
        jnp.concatenate([own, other], axis),
        jnp.concatenate([other, own], axis),
    )


def core_halves(value, axis):
    core = lax.axis_index("core")
    keep = lax.dynamic_index_in_dim(value, core, axis, keepdims=False)
    give = lax.dynamic_index_in_dim(value, 1 - core, axis, keepdims=False)
    return keep, give


def core_summed(value, axis):
    keep, give = core_halves(value, axis)
    return (keep + other_core(give.astype(bf16)).astype(f32)).astype(bf16)


def total(parts):
    return jnp.sum(parts.astype(f32), axis=0)


def dot(left, right, left_dim, right_dim):
    return lax.dot_general(
        left, right, (((left_dim,), (right_dim,)), ((), ())), preferred_element_type=f32
    )


def rotate_rows(first, second, cos, sin):
    return first * cos - second * sin, second * cos + first * sin


def norm_back(normed, root, gain, grad_normed, grad_out):
    weighted = gain * grad_normed
    return (
        grad_out
        + root * weighted
        - normed * root * jnp.mean(normed * weighted, axis=-1, keepdims=True)
    )


def flip(block):
    return block.astype(f32).T.astype(bf16)


def scores_of(keys, query, key_places, query_places, span):
    scores = jnp.dot(keys, query, preferred_element_type=f32)
    places = key_places[span - 512 : span, :]
    visible = jnp.concatenate([places, places], 1) <= query_places
    tail = jnp.where(visible, scores[span - 512 :], -1e30)
    if span == 512:
        return tail
    return jnp.concatenate([scores[: span - 512], tail], 0)


def sort_places(block, rank, places, key_places, query_places):
    row = places[block]
    query_places[rank // 2, :, (rank % 2) * BLOCK : (rank % 2 + 1) * BLOCK] = row
    key_places[rank * BLOCK : (rank + 1) * BLOCK, :] = jnp.broadcast_to(row, (BLOCK, BLOCK)).T


def forward_kernel(
    order, qkv, places, attn, attn_full, log_total, keys, values, query, key_places, query_places
):
    for rank in range(BLOCKS):
        block = order[rank]
        rows = slice(rank * BLOCK, (rank + 1) * BLOCK)
        side = slice((rank % 2) * BLOCK, (rank % 2 + 1) * BLOCK)
        query[rank // 2, :, side] = qkv[block, 0:64, :]
        keys[rows, :] = flip(qkv[block, 64:128, :])
        values[:, rows] = qkv[block, 128:192, :]
        sort_places(block, rank, places, key_places, query_places)
    for quarter in range(4):
        span = 512 * (quarter + 1)

        def pair_step(step, carry, quarter=quarter, span=span):
            pair = 2 * quarter + step
            scores = scores_of(keys[:span, :], query[pair], key_places, query_places[pair], span)
            best = jnp.max(scores, axis=0, keepdims=True)
            weights = jnp.exp(scores - best)
            sums = jnp.sum(weights, axis=0, keepdims=True)
            result = jnp.dot(values[:, :span], weights.astype(bf16), preferred_element_type=f32)
            result = result / sums
            attn_full[pair] = result
            log_total[pair] = best + jnp.log(sums)
            low = result.astype(bf16)
            attn[order[2 * pair]] = low[:, :BLOCK]
            attn[order[2 * pair + 1]] = low[:, BLOCK:]
            return carry

        lax.fori_loop(0, 2, pair_step, 0)


def backward_kernel(
    order,
    qkv,
    places,
    grad_attn,
    attn_full,
    log_total,
    cos,
    sin,
    grad,
    keys,
    keys_wide,
    values,
    query,
    query_tall,
    out_wide,
    out_tall,
    key_places,
    query_places,
    grad_keys,
    grad_values,
):
    for rank in range(BLOCKS):
        block = order[rank]
        rows = slice(rank * BLOCK, (rank + 1) * BLOCK)
        side = slice((rank % 2) * BLOCK, (rank % 2 + 1) * BLOCK)
        query[rank // 2, :, side] = qkv[block, 0:64, :]
        query_tall[rank // 2, side, :] = flip(qkv[block, 0:64, :])
        keys_wide[:, rows] = qkv[block, 64:128, :]
        keys[rows, :] = flip(qkv[block, 64:128, :])
        values[rows, :] = flip(qkv[block, 128:192, :])
        out_wide[rank // 2, :, side] = grad_attn[block]
        out_tall[rank // 2, side, :] = flip(grad_attn[block])
        sort_places(block, rank, places, key_places, query_places)
    grad_keys[...] = jnp.zeros_like(grad_keys)
    grad_values[...] = jnp.zeros_like(grad_values)
    for quarter in range(4):
        span = 512 * (quarter + 1)

        def pair_step(step, carry, quarter=quarter, span=span):
            pair = 2 * quarter + step
            scores = scores_of(keys[:span, :], query[pair], key_places, query_places[pair], span)
            probs = jnp.exp(scores - log_total[pair])
            grad_probs = jnp.dot(values[:span, :], out_wide[pair], preferred_element_type=f32)
            delta = jnp.sum(out_wide[pair].astype(f32) * attn_full[pair], axis=0, keepdims=True)
            grad_scores = (probs * (grad_probs - delta)).astype(bf16)
            grad_query = SCALE * jnp.dot(
                keys_wide[:, :span], grad_scores, preferred_element_type=f32
            )
            grad_keys[:span, :] += jnp.dot(
                grad_scores, query_tall[pair], preferred_element_type=f32
            )
            grad_values[:span, :] += jnp.dot(
                probs.astype(bf16), out_tall[pair], preferred_element_type=f32
            )
            for part in range(2):
                block = order[2 * pair + part]
                piece = grad_query[:, part * BLOCK : (part + 1) * BLOCK]
                first, second = rotate_rows(piece[:HALF], piece[HALF:], cos[block], -sin[block])
                grad[block, 0:32, :] = first.astype(bf16)
                grad[block, 32:64, :] = second.astype(bf16)
            return carry

        lax.fori_loop(0, 2, pair_step, 0)
    for rank in range(BLOCKS):
        block = order[rank]
        rows = slice(rank * BLOCK, (rank + 1) * BLOCK)
        piece = grad_keys[rows, :].T
        first, second = rotate_rows(piece[:HALF], piece[HALF:], cos[block], -sin[block])
        grad[block, 64:96, :] = first.astype(bf16)
        grad[block, 96:128, :] = second.astype(bf16)
        grad[block, 128:192, :] = grad_values[rows, :].T.astype(bf16)


def whole(count):
    return [pl.BlockSpec(memory_space=pltpu.SMEM)] + [pl.BlockSpec(memory_space=pltpu.VMEM)] * count


def attend(order, qkv, places):
    vmem = pl.BlockSpec(memory_space=pltpu.VMEM)
    return pl.pallas_call(
        forward_kernel,
        out_shape=(
            jax.ShapeDtypeStruct((BLOCKS, HEAD_DIM, BLOCK), bf16),
            jax.ShapeDtypeStruct((BLOCKS // 2, HEAD_DIM, PAIR), f32),
            jax.ShapeDtypeStruct((BLOCKS // 2, 1, PAIR), f32),
        ),
        in_specs=whole(2),
        out_specs=(vmem, vmem, vmem),
        scratch_shapes=[
            pltpu.VMEM((LENGTH, HEAD_DIM), bf16),
            pltpu.VMEM((HEAD_DIM, LENGTH), bf16),
            pltpu.VMEM((BLOCKS // 2, HEAD_DIM, PAIR), bf16),
            pltpu.VMEM((LENGTH, BLOCK), f32),
            pltpu.VMEM((BLOCKS // 2, 1, PAIR), f32),
        ],
        compiler_params=pltpu.CompilerParams(vmem_limit_bytes=VMEM_LIMIT),
        name="attend",
    )(order, qkv, places)


def attend_back(order, qkv, places, grad_attn, attn_full, log_total, cos, sin):
    return pl.pallas_call(
        backward_kernel,
        out_shape=jax.ShapeDtypeStruct((BLOCKS, 3 * HEAD_DIM, BLOCK), bf16),
        in_specs=whole(7),
        out_specs=pl.BlockSpec(memory_space=pltpu.VMEM),
        scratch_shapes=[
            pltpu.VMEM((LENGTH, HEAD_DIM), bf16),
            pltpu.VMEM((HEAD_DIM, LENGTH), bf16),
            pltpu.VMEM((LENGTH, HEAD_DIM), bf16),
            pltpu.VMEM((BLOCKS // 2, HEAD_DIM, PAIR), bf16),
            pltpu.VMEM((BLOCKS // 2, PAIR, HEAD_DIM), bf16),
            pltpu.VMEM((BLOCKS // 2, HEAD_DIM, PAIR), bf16),
            pltpu.VMEM((BLOCKS // 2, PAIR, HEAD_DIM), bf16),
            pltpu.VMEM((LENGTH, BLOCK), f32),
            pltpu.VMEM((BLOCKS // 2, 1, PAIR), f32),
            pltpu.VMEM((LENGTH, HEAD_DIM), f32),
            pltpu.VMEM((LENGTH, HEAD_DIM), f32),
        ],
        compiler_params=pltpu.CompilerParams(vmem_limit_bytes=VMEM_LIMIT),
        name="attend_back",
    )(order, qkv, places, grad_attn, attn_full, log_total, cos, sin)


def body(
    inputs,
    positions,
    attn_gain,
    w_query,
    w_key,
    w_value,
    w_out,
    mlp_gain,
    w_gate,
    w_up,
    w_down,
    cotangent,
):
    rows, width = inputs.shape
    shard = w_query.shape[0]
    hidden = w_gate.shape[1] // lax.axis_size("x")
    chips = lax.axis_size("x")

    packed = jnp.concatenate(
        [
            w_query,
            w_key,
            w_value,
            attn_gain[:, None],
            mlp_gain[:, None],
            jnp.zeros((shard, 62), bf16),
        ],
        1,
    )
    packed = lax.all_gather(packed, DP, axis=0, tiled=True)
    qkv_w = packed[:, :QKV]
    gains = packed[:, QKV : QKV + 2].astype(f32).T
    gain_one, gain_two = gains[0:1], gains[1:2]
    all_places = spread(positions[None, :], CTX)
    rank = all_places[:, 0, 0] // BLOCK
    order = jnp.sum(
        jnp.where(
            rank[None, :] == jnp.arange(BLOCKS)[:, None], jnp.arange(BLOCKS)[None, :], 0
        ),
        axis=1,
    ).astype(jnp.int32)
    freq = ROPE_BASE ** (-2.0 * jnp.arange(HALF).astype(f32) / HEAD_DIM)
    places = all_places.astype(f32)
    turns = places * freq[None, :, None]
    cos_all, sin_all = jnp.cos(turns), jnp.sin(turns)
    turn = positions.astype(f32)[None, :] * freq[:, None]
    cos, sin = jnp.cos(turn), jnp.sin(turn)

    resid = inputs.astype(f32)
    root_one = lax.rsqrt(jnp.mean(resid * resid, axis=-1, keepdims=True) + NORM_EPS)
    normed_one = resid * root_one
    hidden_one = (normed_one * gain_one).astype(bf16)

    lin = dot(qkv_w, hidden_one, 0, 1)

    def rotated(part, heads):
        part = part.reshape(heads, 2, HALF, rows)
        first, second = rotate_rows(part[:, 0], part[:, 1], cos, sin)
        return jnp.concatenate([first, second], 1)

    query = (rotated(lin[:Q_WIDTH], HEADS).astype(bf16).astype(f32) * SCALE).astype(bf16)
    keys = rotated(lin[Q_WIDTH : Q_WIDTH + KV_WIDTH], KV_HEADS).astype(bf16)
    values = lin[Q_WIDTH + KV_WIDTH :].astype(bf16).reshape(KV_HEADS, HEAD_DIM, rows)
    chunks = jnp.concatenate(
        [query, jnp.repeat(keys, GROUP, axis=0), jnp.repeat(values, GROUP, axis=0)], 1
    )
    chunks = jnp.concatenate([chunks, jnp.zeros((1, 3 * HEAD_DIM, rows), bf16)], 0)
    gate_up = jnp.concatenate(
        [
            jnp.swapaxes(w_gate.reshape(shard, chips, hidden), 0, 1),
            jnp.swapaxes(w_up.reshape(shard, chips, hidden), 0, 1),
        ],
        2,
    )
    gate_up = exchange(gate_up, "x")
    gate_up_other = other_core(gate_up)
    down_other = other_core(w_down)
    chunks, gate_up, gate_up_other, down_other, order, places, cos_all, sin_all = (
        lax.optimization_barrier(
            (chunks, gate_up, gate_up_other, down_other, order, places, cos_all, sin_all)
        )
    )
    qkv = exchange(chunks, CTX)
    gate_up = core_order(gate_up[:, None], gate_up_other[:, None], 1)
    gate_up = gate_up.reshape(width, 2 * hidden)
    down_w = core_order(w_down, down_other, 0)

    w_out, _ = lax.optimization_barrier((w_out, packed))
    out_w = lax.all_gather(w_out, DP, axis=0, tiled=True)
    dy = jnp.concatenate(from_chips(cotangent), 0)

    attn, attn_full, log_total = attend(order, qkv, places)
    attn_t = exchange(attn, CTX)[:HEADS].reshape(Q_WIDTH, rows)

    mixed = resid + dot(attn_t, out_w, 0, 0)
    root_two = lax.rsqrt(jnp.mean(mixed * mixed, axis=-1, keepdims=True) + NORM_EPS)
    normed_two = mixed * root_two
    hidden_two = (normed_two * gain_two).astype(bf16)
    hidden_two = jnp.concatenate(from_chips(hidden_two), 0)

    early, _ = lax.optimization_barrier((hidden_one, attn_t))
    seq_hidden = lax.all_gather(early, CTX, axis=0, tiled=True).reshape(BLOCKS, rows, width)

    both = dot(hidden_two, gate_up, 1, 0)
    gate, upper = both[:, :hidden], both[:, hidden:]
    sigma = jax.nn.sigmoid(gate)
    silu_gate = gate * sigma
    middle = (silu_gate * upper).astype(bf16)
    grad_middle = dot(dy, down_w, 1, 1)
    grad_both = jnp.concatenate(
        [
            (grad_middle * upper * sigma * (1.0 + gate * (1.0 - sigma))).astype(bf16),
            (grad_middle * silu_gate).astype(bf16),
        ],
        1,
    )
    grad_hidden = to_chips(jnp.split(dot(grad_both, gate_up, 1, 1).astype(bf16), chips))
    out_part = jnp.split(dot(middle, down_w, 1, 0).astype(bf16), chips)

    grad_down = dot(middle, dy, 0, 0)
    grad_gate_up = dot(hidden_two, grad_both, 0, 0)

    grad_mixed = norm_back(normed_two, root_two, gain_two, grad_hidden, cotangent.astype(f32))
    grad_proj = grad_mixed.astype(bf16)
    grad_attn = dot(out_w, grad_proj, 1, 1).astype(bf16).reshape(HEADS, HEAD_DIM, rows)
    grad_attn = jnp.concatenate([grad_attn, jnp.zeros((1, HEAD_DIM, rows), bf16)], 0)
    grad_attn = exchange(grad_attn, CTX)
    grad_out = dot(attn_t, grad_proj, 1, 0)

    output = (mixed + to_chips(out_part)).astype(bf16)

    gd = core_summed(grad_down.reshape(2, hidden // 2, width), 0)
    gg = core_summed(grad_gate_up.reshape(chips, 2, shard, 2 * hidden), 1)
    gg = exchange(gg, "x")
    gg = jnp.swapaxes(gg.reshape(chips, shard, 2, hidden), 0, 1)
    go = core_summed(grad_out.reshape(chips, 2, shard, width), 1)
    go = lax.psum_scatter(
        go.reshape(chips * shard, width), "x", scatter_dimension=0, tiled=True
    )
    sums = lax.psum(
        (
            gg[:, :, 0].reshape(shard, chips * hidden),
            gg[:, :, 1].reshape(shard, chips * hidden),
            gd,
            go,
        ),
        CTX,
    )
    gate_grad, up_grad, down_grad, out_grad = [value.astype(f32) for value in sums]

    grad = attend_back(order, qkv, places, grad_attn, attn_full, log_total, cos_all, sin_all)
    back = exchange(grad, CTX)
    proj_grad = lax.dot_general(
        seq_hidden, grad, (((0, 1), (0, 2)), ((), ())), preferred_element_type=f32
    )
    proj_grad = proj_grad.astype(bf16).reshape(2 * chips, shard, 3 * HEAD_DIM)
    proj_grad = total(exchange(proj_grad, DP)).astype(bf16)
    proj_grad = spread(proj_grad, CTX)[:HEADS].astype(f32)

    def side_by_side(value):
        return jnp.swapaxes(value, 0, 1).reshape(shard, -1)

    query_grad = side_by_side(proj_grad[:, :, :HEAD_DIM])
    grouped = proj_grad.reshape(KV_HEADS, GROUP, shard, 3 * HEAD_DIM)
    kv_grad = grouped[:, 0] + grouped[:, 1] + grouped[:, 2]
    key_grad = side_by_side(kv_grad[:, :, HEAD_DIM : 2 * HEAD_DIM])
    value_grad = side_by_side(kv_grad[:, :, 2 * HEAD_DIM :])

    back = back[:HEADS]
    grad_kv = total(jnp.moveaxis(back[:, HEAD_DIM:].reshape(KV_HEADS, GROUP, 2 * HEAD_DIM, rows), 1, 0))
    grad_kv = grad_kv.astype(bf16)
    grad_lin = jnp.concatenate(
        [
            back[:, :HEAD_DIM].reshape(Q_WIDTH, rows),
            grad_kv[:, :HEAD_DIM].reshape(KV_WIDTH, rows),
            grad_kv[:, HEAD_DIM:].reshape(KV_WIDTH, rows),
        ],
        0,
    )
    grad_hidden_one = dot(grad_lin, qkv_w, 0, 1)
    input_grad = norm_back(normed_one, root_one, gain_one, grad_hidden_one, grad_mixed)

    attn_gain_grad = (
        jnp.sum(w_query.astype(f32) * query_grad, axis=1)
        + jnp.sum(w_key.astype(f32) * key_grad, axis=1)
        + jnp.sum(w_value.astype(f32) * value_grad, axis=1)
    ) / attn_gain.astype(f32)
    mlp_gain_grad = (
        jnp.sum(w_gate.astype(f32) * gate_grad, axis=1)
        + jnp.sum(w_up.astype(f32) * up_grad, axis=1)
    ) / mlp_gain.astype(f32)
    return (
        output,
        input_grad,
        attn_gain_grad,
        query_grad,
        key_grad,
        value_grad,
        out_grad,
        mlp_gain_grad,
        gate_grad,
        up_grad,
        down_grad,
    )


def solution(mesh):
    torus = Mesh(mesh.devices.reshape(4, 2, 4, 4), ALL)
    placed = (
        P(ALL, None),
        P(ALL),
        P(DP),
        P(DP, None),
        P(DP, None),
        P(DP, None),
        P(DP, None),
        P(DP),
        P(DP, None),
        P(DP, None),
        P(DP, None),
        P(ALL, None),
    )
    return jax.shard_map(
        body,
        mesh=torus,
        in_specs=placed,
        out_specs=(
            P(ALL, None),
            P(ALL, None),
            P(DP),
            P(DP, None),
            P(DP, None),
            P(DP, None),
            P(DP, None),
            P(DP),
            P(DP, None),
            P(DP, None),
            P(DP, None),
        ),
        check_vma=False,
    )
```

```python
import jax
import jax.numpy as jnp
from jax import lax
from jax.experimental import pallas as pl
from jax.experimental.pallas import tpu as pltpu
from jax.sharding import Mesh
from jax.sharding import PartitionSpec as P

HEADS = 15
KV_HEADS = 5
GROUP = HEADS // KV_HEADS
HEAD_DIM = 64
HALF = HEAD_DIM // 2
Q_WIDTH = HEADS * HEAD_DIM
KV_WIDTH = KV_HEADS * HEAD_DIM
QKV = Q_WIDTH + 2 * KV_WIDTH
SCALE = HEAD_DIM**-0.5
ROPE_BASE = 100000.0
NORM_EPS = 1e-05
BLOCK = 128
BLOCKS = 16
PAIR = 2 * BLOCK
LENGTH = BLOCK * BLOCKS
PACKED = 1664
SPARE = 8
CHUNK = 3 * HEAD_DIM + 16

DP = ("x", "core")
CTX = ("ctx_0", "ctx_1")
ALL = DP + CTX

f32 = jnp.float32
bf16 = jnp.bfloat16
VMEM_LIMIT = 56 * 1024 * 1024


def exchange(chunks, axis):
    return lax.all_to_all(chunks, axis, split_axis=0, concat_axis=0, tiled=True)


def spread(shard, axis):
    return exchange(jnp.broadcast_to(shard, (lax.axis_size(axis), *shard.shape)), axis)


def other_core(value):
    return lax.ppermute(value, "core", [(0, 1), (1, 0)])


def shift(value, steps):
    return lax.ppermute(value, "x", [(k, (k + steps) % 4) for k in range(4)])


def from_chips(value):
    return [value, shift(value, 1), shift(value, 3), shift(value, 2)]


def to_chips(parts):
    sent = [shift(parts[1], 3), shift(parts[2], 1), shift(parts[3], 2)]
    return parts[0].astype(f32) + sent[0].astype(f32) + sent[1].astype(f32) + sent[2].astype(f32)


def exchange_chips(chunks, chip):
    result = jnp.zeros_like(chunks)
    for steps in range(4):
        part = lax.dynamic_index_in_dim(chunks, (chip + steps) % 4, 0)
        if steps:
            part = shift(part, steps)
        result = lax.dynamic_update_slice_in_dim(result, part, (chip + 4 - steps) % 4, 0)
    return result


def core_order(own, other, axis):
    first = lax.axis_index("core") == 0
    return jnp.where(
        first,
        jnp.concatenate([own, other], axis),
        jnp.concatenate([other, own], axis),
    )


def core_halves(value, axis):
    core = lax.axis_index("core")
    keep = lax.dynamic_index_in_dim(value, core, axis, keepdims=False)
    give = lax.dynamic_index_in_dim(value, 1 - core, axis, keepdims=False)
    return keep, give


def core_summed(value, axis):
    keep, give = core_halves(value, axis)
    return (keep + other_core(give.astype(bf16)).astype(f32)).astype(bf16)


def total(parts):
    return jnp.sum(parts.astype(f32), axis=0)


def dot(left, right, left_dim, right_dim):
    return lax.dot_general(
        left, right, (((left_dim,), (right_dim,)), ((), ())), preferred_element_type=f32
    )


def rotate_rows(first, second, cos, sin):
    return first * cos - second * sin, second * cos + first * sin


def norm_back(normed, root, gain, grad_normed, grad_out):
    weighted = gain * grad_normed
    return (
        grad_out
        + root * weighted
        - normed * root * jnp.mean(normed * weighted, axis=-1, keepdims=True)
    )


def flip(block):
    return block.astype(f32).T.astype(bf16)


def scores_of(keys, query, key_places, query_places, span):
    scores = jnp.dot(keys, query, preferred_element_type=f32)
    places = key_places[span - 512 : span, :]
    visible = jnp.concatenate([places, places], 1) <= query_places
    tail = jnp.where(visible, scores[span - 512 :], -1e30)
    if span == 512:
        return tail
    return jnp.concatenate([scores[: span - 512], tail], 0)


def sort_places(block, rank, places, key_places, query_places):
    row = places[block]
    query_places[rank // 2, :, (rank % 2) * BLOCK : (rank % 2 + 1) * BLOCK] = row
    key_places[rank * BLOCK : (rank + 1) * BLOCK, :] = jnp.broadcast_to(row, (BLOCK, BLOCK)).T


def forward_kernel(
    order, qkv, places, attn, attn_full, log_total, keys, values, query, key_places, query_places
):
    for rank in range(BLOCKS):
        block = order[rank]
        rows = slice(rank * BLOCK, (rank + 1) * BLOCK)
        side = slice((rank % 2) * BLOCK, (rank % 2 + 1) * BLOCK)
        query[rank // 2, :, side] = qkv[block, 0:64, :]
        keys[rows, :] = flip(qkv[block, 64:128, :])
        values[:, rows] = qkv[block, 128:192, :]
        sort_places(block, rank, places, key_places, query_places)
    for quarter in range(4):
        span = 512 * (quarter + 1)

        def pair_step(step, carry, quarter=quarter, span=span):
            pair = 2 * quarter + step
            scores = scores_of(keys[:span, :], query[pair], key_places, query_places[pair], span)
            best = jnp.max(scores, axis=0, keepdims=True)
            weights = jnp.exp(scores - best)
            sums = jnp.sum(weights, axis=0, keepdims=True)
            result = jnp.dot(values[:, :span], weights.astype(bf16), preferred_element_type=f32)
            result = result / sums
            attn_full[pair] = result
            log_total[pair] = best + jnp.log(sums)
            low = result.astype(bf16)
            attn[order[2 * pair]] = low[:, :BLOCK]
            attn[order[2 * pair + 1]] = low[:, BLOCK:]
            return carry

        lax.fori_loop(0, 2, pair_step, 0)


def backward_kernel(
    order,
    qkv,
    places,
    grad_attn,
    attn_full,
    log_total,
    cos,
    sin,
    grad,
    keys,
    keys_wide,
    values,
    query,
    query_tall,
    out_wide,
    out_tall,
    key_places,
    query_places,
    grad_keys,
    grad_values,
):
    for rank in range(BLOCKS):
        block = order[rank]
        rows = slice(rank * BLOCK, (rank + 1) * BLOCK)
        side = slice((rank % 2) * BLOCK, (rank % 2 + 1) * BLOCK)
        query[rank // 2, :, side] = qkv[block, 0:64, :]
        query_tall[rank // 2, side, :] = flip(qkv[block, 0:64, :])
        keys_wide[:, rows] = qkv[block, 64:128, :]
        keys[rows, :] = flip(qkv[block, 64:128, :])
        values[rows, :] = flip(qkv[block, 128:192, :])
        out_wide[rank // 2, :, side] = grad_attn[block]
        out_tall[rank // 2, side, :] = flip(grad_attn[block])
        sort_places(block, rank, places, key_places, query_places)
    grad_keys[...] = jnp.zeros_like(grad_keys)
    grad_values[...] = jnp.zeros_like(grad_values)
    for quarter in range(4):
        span = 512 * (quarter + 1)

        def pair_step(step, carry, quarter=quarter, span=span):
            pair = 2 * quarter + step
            scores = scores_of(keys[:span, :], query[pair], key_places, query_places[pair], span)
            probs = jnp.exp(scores - log_total[pair])
            grad_probs = jnp.dot(values[:span, :], out_wide[pair], preferred_element_type=f32)
            delta = jnp.sum(out_wide[pair].astype(f32) * attn_full[pair], axis=0, keepdims=True)
            grad_scores = (probs * (grad_probs - delta)).astype(bf16)
            grad_query = SCALE * jnp.dot(
                keys_wide[:, :span], grad_scores, preferred_element_type=f32
            )
            grad_keys[:span, :] += jnp.dot(
                grad_scores, query_tall[pair], preferred_element_type=f32
            )
            grad_values[:span, :] += jnp.dot(
                probs.astype(bf16), out_tall[pair], preferred_element_type=f32
            )
            for part in range(2):
                block = order[2 * pair + part]
                piece = grad_query[:, part * BLOCK : (part + 1) * BLOCK]
                first, second = rotate_rows(piece[:HALF], piece[HALF:], cos[block], -sin[block])
                grad[block, 0:32, :] = first.astype(bf16)
                grad[block, 32:64, :] = second.astype(bf16)
            return carry

        lax.fori_loop(0, 2, pair_step, 0)
    for rank in range(BLOCKS):
        block = order[rank]
        rows = slice(rank * BLOCK, (rank + 1) * BLOCK)
        piece = grad_keys[rows, :].T
        first, second = rotate_rows(piece[:HALF], piece[HALF:], cos[block], -sin[block])
        grad[block, 64:96, :] = first.astype(bf16)
        grad[block, 96:128, :] = second.astype(bf16)
        grad[block, 128:192, :] = grad_values[rows, :].T.astype(bf16)


def grads_kernel(core, hidden, grad_both, middle, dy, keep, give, wide, tall):
    width, span = hidden.shape[1], grad_both.shape[1]
    units = middle.shape[1]
    wide[0:width, :] = lax.dot_general(
        hidden[...], grad_both[...], (((0,), (0,)), ((), ())), preferred_element_type=f32
    )
    wide[width : width + 8, :] = jnp.zeros((8, span), f32)
    tall[...] = jnp.zeros_like(tall)
    tall[0:units, 0:width] = lax.dot_general(
        middle[...], dy[...], (((0,), (0,)), ((), ())), preferred_element_type=f32
    )
    shard = width // 8
    for target, side in ((keep, core[0]), (give, 1 - core[0])):

        def step(piece, carry, target=target, side=side):
            for chip in range(4):
                start = pl.multiple_of((2 * chip + side) * shard + 16 * piece, 8)
                target[piece, :, chip * span : (chip + 1) * span] = wide[pl.ds(start, 16), :].astype(
                    bf16
                )
            for part in range(3):
                start = pl.multiple_of(side * (units // 2) + 48 * piece + 8 * part, 8)
                upper = tall[pl.ds(start, 8), :]
                lower = tall[pl.ds(pl.multiple_of(start + 24, 8), 8), :]
                at = 4 * span + part * 1024
                target[piece, :, at : at + 1024] = jnp.concatenate([upper, lower], 0).astype(bf16)
            return carry

        lax.fori_loop(0, 8, step, 0)


def feed_forward_grads(core, hidden, grad_both, middle, dy):
    vmem = pl.BlockSpec(memory_space=pltpu.VMEM)
    span = 4 * grad_both.shape[1] + 3 * 1024
    return pl.pallas_call(
        grads_kernel,
        out_shape=(jax.ShapeDtypeStruct((8, 16, span), bf16),) * 2,
        in_specs=whole(4),
        out_specs=(vmem, vmem),
        scratch_shapes=[
            pltpu.VMEM((hidden.shape[1] + 8, grad_both.shape[1]), f32),
            pltpu.VMEM((middle.shape[1] + 64, 1024), f32),
        ],
        compiler_params=pltpu.CompilerParams(vmem_limit_bytes=VMEM_LIMIT),
        name="feed_forward_grads",
    )(core, hidden, grad_both, middle, dy)


def whole(count):
    return [pl.BlockSpec(memory_space=pltpu.SMEM)] + [pl.BlockSpec(memory_space=pltpu.VMEM)] * count


def attend(order, qkv, places):
    vmem = pl.BlockSpec(memory_space=pltpu.VMEM)
    return pl.pallas_call(
        forward_kernel,
        out_shape=(
            jax.ShapeDtypeStruct((BLOCKS, HEAD_DIM, BLOCK), bf16),
            jax.ShapeDtypeStruct((BLOCKS // 2, HEAD_DIM, PAIR), f32),
            jax.ShapeDtypeStruct((BLOCKS // 2, 1, PAIR), f32),
        ),
        in_specs=whole(2),
        out_specs=(vmem, vmem, vmem),
        scratch_shapes=[
            pltpu.VMEM((LENGTH, HEAD_DIM), bf16),
            pltpu.VMEM((HEAD_DIM, LENGTH), bf16),
            pltpu.VMEM((BLOCKS // 2, HEAD_DIM, PAIR), bf16),
            pltpu.VMEM((LENGTH, BLOCK), f32),
            pltpu.VMEM((BLOCKS // 2, 1, PAIR), f32),
        ],
        compiler_params=pltpu.CompilerParams(vmem_limit_bytes=VMEM_LIMIT),
        name="attend",
    )(order, qkv, places)


def attend_back(order, qkv, places, grad_attn, attn_full, log_total, cos, sin):
    return pl.pallas_call(
        backward_kernel,
        out_shape=jax.ShapeDtypeStruct((BLOCKS, 3 * HEAD_DIM, BLOCK), bf16),
        in_specs=whole(7),
        out_specs=pl.BlockSpec(memory_space=pltpu.VMEM),
        scratch_shapes=[
            pltpu.VMEM((LENGTH, HEAD_DIM), bf16),
            pltpu.VMEM((HEAD_DIM, LENGTH), bf16),
            pltpu.VMEM((LENGTH, HEAD_DIM), bf16),
            pltpu.VMEM((BLOCKS // 2, HEAD_DIM, PAIR), bf16),
            pltpu.VMEM((BLOCKS // 2, PAIR, HEAD_DIM), bf16),
            pltpu.VMEM((BLOCKS // 2, HEAD_DIM, PAIR), bf16),
            pltpu.VMEM((BLOCKS // 2, PAIR, HEAD_DIM), bf16),
            pltpu.VMEM((LENGTH, BLOCK), f32),
            pltpu.VMEM((BLOCKS // 2, 1, PAIR), f32),
            pltpu.VMEM((LENGTH, HEAD_DIM), f32),
            pltpu.VMEM((LENGTH, HEAD_DIM), f32),
        ],
        compiler_params=pltpu.CompilerParams(vmem_limit_bytes=VMEM_LIMIT),
        name="attend_back",
    )(order, qkv, places, grad_attn, attn_full, log_total, cos, sin)


def body(
    inputs,
    positions,
    attn_gain,
    w_query,
    w_key,
    w_value,
    w_out,
    mlp_gain,
    w_gate,
    w_up,
    w_down,
    cotangent,
):
    rows, width = inputs.shape
    shard = w_query.shape[0]
    hidden = w_gate.shape[1] // lax.axis_size("x")
    chips = lax.axis_size("x")

    chip = lax.axis_index("x")
    core = lax.axis_index("core")

    spare = jnp.zeros((1, SPARE), bf16)
    gain_row = jnp.concatenate(
        [attn_gain[None, :], spare, mlp_gain[None, :], jnp.zeros((1, PACKED - 2 * BLOCK + SPARE), bf16)],
        1,
    )
    packed = jnp.concatenate(
        [
            jnp.concatenate([w_query, w_key, w_value, jnp.zeros((shard, PACKED - QKV), bf16)], 1),
            gain_row,
            jnp.zeros((SPARE - 1, PACKED), bf16),
        ],
        0,
    )
    own_w = spread(packed, "x")
    gate_up = jnp.concatenate(
        [
            jnp.swapaxes(w_gate.reshape(shard, chips, hidden), 0, 1),
            jnp.swapaxes(w_up.reshape(shard, chips, hidden), 0, 1),
        ],
        2,
    )
    own_w, gate_up = lax.optimization_barrier((own_w, gate_up))
    other_w = other_core(own_w)
    gain_rows = core_order(own_w[:, None, shard, :], other_w[:, None, shard, :], 1)
    gain_rows = gain_rows.reshape(2 * chips, PACKED).astype(f32)
    gain_one = gain_rows[:, :shard].reshape(1, width)
    gain_two = gain_rows[:, BLOCK : BLOCK + shard].reshape(1, width)
    own_w = own_w.reshape(chips * BLOCK, PACKED)
    other_w = other_w.reshape(chips * BLOCK, PACKED)

    freq = ROPE_BASE ** (-2.0 * jnp.arange(HALF).astype(f32) / HEAD_DIM)
    turn = positions.astype(f32)[None, :] * freq[:, None]
    cos, sin = jnp.cos(turn), jnp.sin(turn)

    resid = inputs.astype(f32)
    root_one = lax.rsqrt(jnp.mean(resid * resid, axis=-1, keepdims=True) + NORM_EPS)
    normed_one = resid * root_one
    hidden_one = (normed_one * gain_one).astype(bf16)

    columns = hidden_one.T.reshape(chips, 2, shard, rows)
    columns = jnp.pad(columns, ((0, 0), (0, 0), (0, SPARE), (0, 0)))
    own_columns, other_columns = core_halves(columns, 1)
    lin = dot(own_w, own_columns.reshape(chips * BLOCK, rows), 0, 0) + dot(
        other_w, other_columns.reshape(chips * BLOCK, rows), 0, 0
    )

    def rotated(part, heads):
        part = part.reshape(heads, 2, HALF, rows)
        first, second = rotate_rows(part[:, 0], part[:, 1], cos, sin)
        return jnp.concatenate([first, second], 1)

    query = (rotated(lin[:Q_WIDTH], HEADS).astype(bf16).astype(f32) * SCALE).astype(bf16)
    keys = rotated(lin[Q_WIDTH : Q_WIDTH + KV_WIDTH], KV_HEADS).astype(bf16)
    values = lin[Q_WIDTH + KV_WIDTH : QKV].astype(bf16).reshape(KV_HEADS, HEAD_DIM, rows)
    chunks = jnp.concatenate(
        [query, jnp.repeat(keys, GROUP, axis=0), jnp.repeat(values, GROUP, axis=0)], 1
    )
    chunks = jnp.concatenate([chunks, jnp.zeros((1, 3 * HEAD_DIM, rows), bf16)], 0)
    place_rows = jnp.stack([positions // BLOCK, positions % BLOCK]).astype(bf16)
    place_rows = jnp.pad(place_rows, ((0, 14), (0, 0)))
    chunks = jnp.concatenate(
        [chunks, jnp.broadcast_to(place_rows, (BLOCKS, 16, rows))], 1
    )
    qkv = exchange(chunks, CTX)
    rank = qkv[:, 3 * HEAD_DIM, 0].astype(jnp.int32)
    order = jnp.sum(
        jnp.where(
            rank[None, :] == jnp.arange(BLOCKS)[:, None], jnp.arange(BLOCKS)[None, :], 0
        ),
        axis=1,
    ).astype(jnp.int32)
    places = qkv[:, 192:193].astype(f32) * float(BLOCK) + qkv[:, 193:194].astype(f32)

    w_out, _ = lax.optimization_barrier((w_out, own_w))
    out_w = lax.all_gather(w_out, DP, axis=0, tiled=True)
    w_down_late, dy, gate_up, _ = lax.optimization_barrier((w_down, cotangent, gate_up, qkv))
    gate_up = exchange(gate_up, "x")
    turns = places * freq[None, :, None]
    cos_all, sin_all = jnp.cos(turns), jnp.sin(turns)

    attn, attn_full, log_total = attend(order, qkv, places)
    attn, gate_up = lax.optimization_barrier((attn, gate_up))
    gate_up = core_order(gate_up[:, None], other_core(gate_up)[:, None], 1)
    gate_up = gate_up.reshape(width, 2 * hidden)
    down_w = core_order(w_down_late, other_core(w_down_late), 0)
    dy = jnp.concatenate(from_chips(dy), 0)
    attn_t = exchange(attn, CTX)
    attn_t, cos_all, sin_all = lax.optimization_barrier((attn_t, cos_all, sin_all))
    attn_t = attn_t[:HEADS].reshape(Q_WIDTH, rows)

    mixed = resid + dot(attn_t, out_w, 0, 0)
    root_two = lax.rsqrt(jnp.mean(mixed * mixed, axis=-1, keepdims=True) + NORM_EPS)
    normed_two = mixed * root_two
    hidden_two = (normed_two * gain_two).astype(bf16)
    hidden_two = jnp.concatenate(from_chips(hidden_two), 0)

    early, _ = lax.optimization_barrier((hidden_one, qkv))
    seq_hidden = lax.all_gather(early, CTX, axis=0, tiled=True).reshape(BLOCKS, rows, width)

    both = dot(hidden_two, gate_up, 1, 0)
    gate, upper = both[:, :hidden], both[:, hidden:]
    sigma = jax.nn.sigmoid(gate)
    silu_gate = gate * sigma
    middle = (silu_gate * upper).astype(bf16)
    grad_middle = dot(dy, down_w, 1, 1)
    grad_both = jnp.concatenate(
        [
            (grad_middle * upper * sigma * (1.0 + gate * (1.0 - sigma))).astype(bf16),
            (grad_middle * silu_gate).astype(bf16),
        ],
        1,
    )
    grad_hidden = dot(grad_both, gate_up, 1, 1).astype(bf16)
    middle, grad_both, _ = lax.optimization_barrier((middle, grad_both, grad_hidden))
    grad_hidden = to_chips(jnp.split(grad_hidden, chips))

    keep, give = feed_forward_grads(core[None], hidden_two, grad_both, middle, dy)
    pieces = (keep.astype(f32) + other_core(give).astype(f32)).astype(bf16)
    grad_hidden, pieces, seq_hidden = lax.optimization_barrier((grad_hidden, pieces, seq_hidden))
    pieces = exchange(pieces.reshape(BLOCKS, 8, -1), CTX)

    grad_mixed = norm_back(normed_two, root_two, gain_two, grad_hidden, cotangent.astype(f32))
    grad_proj = grad_mixed.astype(bf16)
    grad_attn = dot(out_w, grad_proj, 1, 1).astype(bf16).reshape(HEADS, HEAD_DIM, rows)
    grad_attn = jnp.concatenate([grad_attn, jnp.zeros((1, HEAD_DIM, rows), bf16)], 0)
    grad_attn, pieces, late_proj = lax.optimization_barrier((grad_attn, pieces, grad_proj))
    grad_attn = exchange(grad_attn, CTX)

    own_attn, other_attn = core_halves(attn_t.reshape(chips, 2, shard, rows), 1)
    own_attn, other_attn = [
        dot(part.reshape(chips * shard, rows), late_proj, 1, 0) for part in (own_attn, other_attn)
    ]
    go = (own_attn + other_core(other_attn.astype(bf16)).astype(f32)).astype(bf16)
    go = go.reshape(chips, shard, width)
    go = to_chips(
        [
            lax.dynamic_index_in_dim(go, (chip + steps) % 4, 0, keepdims=False)
            for steps in (0, 3, 1, 2)
        ]
    ).astype(bf16)

    pieces = total(pieces).astype(bf16)
    share = 2 * hidden
    mine = exchange(
        jnp.stack([pieces[:, k * share : (k + 1) * share] for k in range(4)]), "x"
    )
    mine = jnp.concatenate(
        [mine[k, :, :hidden] for k in range(4)]
        + [mine[k, :, hidden:] for k in range(4)]
        + [pieces[:, chips * share :]],
        1,
    )
    mine = lax.all_gather(mine, CTX, axis=0, tiled=True)
    wide = chips * hidden
    gate_grad = mine[:shard, :wide].astype(f32)
    up_grad = mine[:shard, wide : 2 * wide].astype(f32)
    down_grad = jnp.swapaxes(mine[:, 2 * wide :].reshape(BLOCKS, 8, 3, 1024), 1, 2)
    down_grad = down_grad.reshape(24 * BLOCKS, 1024)[: hidden // 2, :width].astype(f32)

    grad = attend_back(order, qkv, places, grad_attn, attn_full, log_total, cos_all, sin_all)
    go = jnp.pad(go, ((0, SPARE), (0, 0))).reshape(BLOCKS, 8 * width // BLOCK, BLOCK)
    go = jnp.pad(go, ((0, 0), (0, 4), (0, 0)))
    back = exchange(jnp.concatenate([grad, go], 1), CTX)
    early_middle, _ = lax.optimization_barrier((middle, grad))
    out_part = jnp.split(dot(early_middle, down_w, 1, 0).astype(bf16), chips)
    output = (mixed + to_chips(out_part)).astype(bf16)
    proj_grad = lax.dot_general(
        seq_hidden, grad, (((0, 1), (0, 2)), ((), ())), preferred_element_type=f32
    )
    proj_grad = proj_grad.astype(bf16).reshape(2 * chips, shard, 3 * HEAD_DIM)
    proj_grad, back = lax.optimization_barrier((proj_grad, back))
    proj_grad = total(exchange(proj_grad, DP)).astype(bf16)
    go = total(back[:, 3 * HEAD_DIM : 3 * HEAD_DIM + 8 * width // BLOCK]).astype(bf16)
    proj_grad = spread(
        jnp.concatenate([proj_grad, go.reshape(shard, 8 * width // shard)], 1), CTX
    ).astype(f32)
    out_grad = proj_grad[:, :, 3 * HEAD_DIM :].reshape(BLOCKS * 8, width)[:shard]
    proj_grad = proj_grad[:HEADS, :, : 3 * HEAD_DIM]

    def side_by_side(value):
        return jnp.swapaxes(value, 0, 1).reshape(shard, -1)

    query_grad = side_by_side(proj_grad[:, :, :HEAD_DIM])
    grouped = proj_grad.reshape(KV_HEADS, GROUP, shard, 3 * HEAD_DIM)
    kv_grad = grouped[:, 0] + grouped[:, 1] + grouped[:, 2]
    key_grad = side_by_side(kv_grad[:, :, HEAD_DIM : 2 * HEAD_DIM])
    value_grad = side_by_side(kv_grad[:, :, 2 * HEAD_DIM :])

    back = back[:HEADS]
    grad_kv = total(jnp.moveaxis(back[:, HEAD_DIM : 3 * HEAD_DIM].reshape(KV_HEADS, GROUP, 2 * HEAD_DIM, rows), 1, 0))
    grad_kv = grad_kv.astype(bf16)
    grad_lin = jnp.concatenate(
        [
            back[:, :HEAD_DIM].reshape(Q_WIDTH, rows),
            grad_kv[:, :HEAD_DIM].reshape(KV_WIDTH, rows),
            grad_kv[:, HEAD_DIM:].reshape(KV_WIDTH, rows),
            jnp.zeros((PACKED - QKV, rows), bf16),
        ],
        0,
    )
    own_grad = dot(own_w, grad_lin, 1, 0).reshape(chips, 1, BLOCK, rows)[:, :, :shard]
    other_grad = dot(other_w, grad_lin, 1, 0).reshape(chips, 1, BLOCK, rows)[:, :, :shard]
    grad_hidden_one = core_order(own_grad, other_grad, 1).reshape(width, rows).T
    input_grad = norm_back(normed_one, root_one, gain_one, grad_hidden_one, grad_mixed)

    attn_gain_grad = (
        jnp.sum(w_query.astype(f32) * query_grad, axis=1)
        + jnp.sum(w_key.astype(f32) * key_grad, axis=1)
        + jnp.sum(w_value.astype(f32) * value_grad, axis=1)
    ) / attn_gain.astype(f32)
    mlp_gain_grad = (
        jnp.sum(w_gate.astype(f32) * gate_grad, axis=1)
        + jnp.sum(w_up.astype(f32) * up_grad, axis=1)
    ) / mlp_gain.astype(f32)
    return (
        output,
        input_grad,
        attn_gain_grad,
        query_grad,
        key_grad,
        value_grad,
        out_grad,
        mlp_gain_grad,
        gate_grad,
        up_grad,
        down_grad,
    )


def solution(mesh):
    torus = Mesh(mesh.devices.reshape(4, 2, 4, 4), ALL)
    placed = (
        P(ALL, None),
        P(ALL),
        P(DP),
        P(DP, None),
        P(DP, None),
        P(DP, None),
        P(DP, None),
        P(DP),
        P(DP, None),
        P(DP, None),
        P(DP, None),
        P(ALL, None),
    )
    return jax.shard_map(
        body,
        mesh=torus,
        in_specs=placed,
        out_specs=(
            P(ALL, None),
            P(ALL, None),
            P(DP),
            P(DP, None),
            P(DP, None),
            P(DP, None),
            P(DP, None),
            P(DP),
            P(DP, None),
            P(DP, None),
            P(DP, None),
        ),
        check_vma=False,
    )
```

```python
import jax
import jax.numpy as jnp
from jax import lax
from jax.experimental import pallas as pl
from jax.experimental.pallas import tpu as pltpu
from jax.sharding import Mesh
from jax.sharding import PartitionSpec as P

HEADS = 15
KV_HEADS = 5
GROUP = HEADS // KV_HEADS
HEAD_DIM = 64
HALF = HEAD_DIM // 2
Q_WIDTH = HEADS * HEAD_DIM
KV_WIDTH = KV_HEADS * HEAD_DIM
QKV = Q_WIDTH + 2 * KV_WIDTH
SCALE = HEAD_DIM**-0.5
ROPE_BASE = 100000.0
NORM_EPS = 1e-05
BLOCK = 128
BLOCKS = 16
PAIR = 2 * BLOCK
LENGTH = BLOCK * BLOCKS
PACKED = 1664
SPARE = 8
CHUNK = 3 * HEAD_DIM + 16

DP = ("x", "core")
CTX = ("ctx_0", "ctx_1")
ALL = DP + CTX

f32 = jnp.float32
bf16 = jnp.bfloat16
VMEM_LIMIT = 56 * 1024 * 1024


def exchange(chunks, axis):
    return lax.all_to_all(chunks, axis, split_axis=0, concat_axis=0, tiled=True)


def spread(shard, axis):
    return exchange(jnp.broadcast_to(shard, (lax.axis_size(axis), *shard.shape)), axis)


def other_core(value):
    return lax.ppermute(value, "core", [(0, 1), (1, 0)])


def shift(value, steps, axis="x"):
    return lax.ppermute(value, axis, [(k, (k + steps) % 4) for k in range(4)])


def received(parts, axis):
    return [parts[0]] + [shift(parts[k], k, axis) for k in (1, 3, 2)]


def from_chips(value):
    return [value, shift(value, 1), shift(value, 3), shift(value, 2)]


def parts_of(parts):
    return [parts[0], shift(parts[1], 3), shift(parts[2], 1), shift(parts[3], 2)]


def to_chips(parts):
    sent = parts_of(parts)
    return sent[0].astype(f32) + sent[1].astype(f32) + sent[2].astype(f32) + sent[3].astype(f32)


def exchange_chips(chunks, chip):
    result = jnp.zeros_like(chunks)
    for steps in range(4):
        part = lax.dynamic_index_in_dim(chunks, (chip + steps) % 4, 0)
        if steps:
            part = shift(part, steps)
        result = lax.dynamic_update_slice_in_dim(result, part, (chip + 4 - steps) % 4, 0)
    return result


def summed_over(chunks, axis):
    me = lax.axis_index(axis)
    parts = [
        lax.dynamic_index_in_dim(chunks, (me + k) % 4, 0, keepdims=False) for k in range(4)
    ]
    return sum(part.astype(f32) for part in received(parts, axis)).astype(bf16)


def core_order(own, other, axis):
    first = lax.axis_index("core") == 0
    return jnp.where(
        first,
        jnp.concatenate([own, other], axis),
        jnp.concatenate([other, own], axis),
    )


def core_halves(value, axis):
    core = lax.axis_index("core")
    keep = lax.dynamic_index_in_dim(value, core, axis, keepdims=False)
    give = lax.dynamic_index_in_dim(value, 1 - core, axis, keepdims=False)
    return keep, give


def core_summed(value, axis):
    keep, give = core_halves(value, axis)
    return (keep + other_core(give.astype(bf16)).astype(f32)).astype(bf16)


def total(parts):
    return jnp.sum(parts.astype(f32), axis=0)


def dot(left, right, left_dim, right_dim):
    return lax.dot_general(
        left, right, (((left_dim,), (right_dim,)), ((), ())), preferred_element_type=f32
    )


def rotate_rows(first, second, cos, sin):
    return first * cos - second * sin, second * cos + first * sin


def norm_back(normed, root, gain, grad_normed, grad_out):
    weighted = gain * grad_normed
    return (
        grad_out
        + root * weighted
        - normed * root * jnp.mean(normed * weighted, axis=-1, keepdims=True)
    )


def flip(block):
    return block.astype(f32).T.astype(bf16)


def scores_of(keys, query, key_places, query_places, span):
    scores = jnp.dot(keys, query, preferred_element_type=f32)
    places = key_places[span - 512 : span, :]
    visible = jnp.concatenate([places, places], 1) <= query_places
    tail = jnp.where(visible, scores[span - 512 :], -1e30)
    if span == 512:
        return tail
    return jnp.concatenate([scores[: span - 512], tail], 0)


def sort_places(block, rank, places, key_places, query_places):
    row = places[block]
    query_places[rank // 2, :, (rank % 2) * BLOCK : (rank % 2 + 1) * BLOCK] = row
    key_places[rank * BLOCK : (rank + 1) * BLOCK, :] = jnp.broadcast_to(row, (BLOCK, BLOCK)).T


def forward_kernel(
    order, qkv, places, attn, attn_full, log_total, keys, values, query, key_places, query_places
):
    for rank in range(BLOCKS):
        block = order[rank]
        rows = slice(rank * BLOCK, (rank + 1) * BLOCK)
        side = slice((rank % 2) * BLOCK, (rank % 2 + 1) * BLOCK)
        query[rank // 2, :, side] = qkv[block, 0:64, :]
        keys[rows, :] = flip(qkv[block, 64:128, :])
        values[:, rows] = qkv[block, 128:192, :]
        sort_places(block, rank, places, key_places, query_places)
    for quarter in range(4):
        span = 512 * (quarter + 1)

        def pair_step(step, carry, quarter=quarter, span=span):
            pair = 2 * quarter + step
            scores = scores_of(keys[:span, :], query[pair], key_places, query_places[pair], span)
            best = jnp.max(scores, axis=0, keepdims=True)
            weights = jnp.exp(scores - best)
            sums = jnp.sum(weights, axis=0, keepdims=True)
            result = jnp.dot(values[:, :span], weights.astype(bf16), preferred_element_type=f32)
            result = result / sums
            attn_full[pair] = result
            log_total[pair] = best + jnp.log(sums)
            low = result.astype(bf16)
            attn[order[2 * pair]] = low[:, :BLOCK]
            attn[order[2 * pair + 1]] = low[:, BLOCK:]
            return carry

        lax.fori_loop(0, 2, pair_step, 0)


def backward_kernel(
    order,
    qkv,
    places,
    grad_attn,
    attn_full,
    log_total,
    cos,
    sin,
    grad,
    keys,
    keys_wide,
    values,
    query,
    query_tall,
    out_wide,
    out_tall,
    key_places,
    query_places,
    grad_keys,
    grad_values,
):
    for rank in range(BLOCKS):
        block = order[rank]
        rows = slice(rank * BLOCK, (rank + 1) * BLOCK)
        side = slice((rank % 2) * BLOCK, (rank % 2 + 1) * BLOCK)
        query[rank // 2, :, side] = qkv[block, 0:64, :]
        query_tall[rank // 2, side, :] = flip(qkv[block, 0:64, :])
        keys_wide[:, rows] = qkv[block, 64:128, :]
        keys[rows, :] = flip(qkv[block, 64:128, :])
        values[rows, :] = flip(qkv[block, 128:192, :])
        out_wide[rank // 2, :, side] = grad_attn[block]
        out_tall[rank // 2, side, :] = flip(grad_attn[block])
        sort_places(block, rank, places, key_places, query_places)
    grad_keys[...] = jnp.zeros_like(grad_keys)
    grad_values[...] = jnp.zeros_like(grad_values)
    for quarter in range(4):
        span = 512 * (quarter + 1)

        def pair_step(step, carry, quarter=quarter, span=span):
            pair = 2 * quarter + step
            scores = scores_of(keys[:span, :], query[pair], key_places, query_places[pair], span)
            probs = jnp.exp(scores - log_total[pair])
            grad_probs = jnp.dot(values[:span, :], out_wide[pair], preferred_element_type=f32)
            delta = jnp.sum(out_wide[pair].astype(f32) * attn_full[pair], axis=0, keepdims=True)
            grad_scores = (probs * (grad_probs - delta)).astype(bf16)
            grad_query = SCALE * jnp.dot(
                keys_wide[:, :span], grad_scores, preferred_element_type=f32
            )
            grad_keys[:span, :] += jnp.dot(
                grad_scores, query_tall[pair], preferred_element_type=f32
            )
            grad_values[:span, :] += jnp.dot(
                probs.astype(bf16), out_tall[pair], preferred_element_type=f32
            )
            for part in range(2):
                block = order[2 * pair + part]
                piece = grad_query[:, part * BLOCK : (part + 1) * BLOCK]
                first, second = rotate_rows(piece[:HALF], piece[HALF:], cos[block], -sin[block])
                grad[block, 0:32, :] = first.astype(bf16)
                grad[block, 32:64, :] = second.astype(bf16)
            return carry

        lax.fori_loop(0, 2, pair_step, 0)
    for rank in range(BLOCKS):
        block = order[rank]
        rows = slice(rank * BLOCK, (rank + 1) * BLOCK)
        piece = grad_keys[rows, :].T
        first, second = rotate_rows(piece[:HALF], piece[HALF:], cos[block], -sin[block])
        grad[block, 64:96, :] = first.astype(bf16)
        grad[block, 96:128, :] = second.astype(bf16)
        grad[block, 128:192, :] = grad_values[rows, :].T.astype(bf16)


def grads_kernel(place, hidden, grad_both, middle, dy, keep, give, wide, tall):
    width, span = hidden.shape[1], grad_both.shape[1]
    units = middle.shape[1]
    wide[0:width, :] = lax.dot_general(
        hidden[...], grad_both[...], (((0,), (0,)), ((), ())), preferred_element_type=f32
    )
    wide[width : width + 8, :] = jnp.zeros((8, span), f32)
    tall[...] = jnp.zeros_like(tall)
    tall[0:units, 0:width] = lax.dot_general(
        middle[...], dy[...], (((0,), (0,)), ((), ())), preferred_element_type=f32
    )
    shard = width // 8
    half = span // 2
    for target, side in ((keep, place[1]), (give, 1 - place[1])):

        def step(piece, carry, target=target, side=side):
            first, second = piece // 4, piece % 4
            for part in range(7):
                if part < 4:
                    start = (2 * part + side) * shard + 8 * piece
                    block = wide[pl.ds(pl.multiple_of(start, 8), 8), :]
                    slot = (part + 4 - place[0]) % 4
                else:
                    start = side * (units // 2) + 24 * piece + 8 * (part - 4)
                    block = tall[pl.ds(pl.multiple_of(start, 8), 8), :]
                    slot = part
                target[second, first, pl.ds(pl.multiple_of(16 * slot, 16), 16), :] = (
                    jnp.concatenate([block[:, :half], block[:, half:]], 0).astype(bf16)
                )
            return carry

        lax.fori_loop(0, BLOCKS, step, 0)


def unpack_kernel(
    place,
    pieces,
    side,
    w_query,
    w_key,
    w_value,
    w_gate,
    w_up,
    gains,
    query,
    key,
    value,
    out,
    gate,
    up,
    down,
    gain_grads,
):
    half = gate.shape[1] // 4
    rows = query.shape[0]
    width = down.shape[1]
    for piece in range(BLOCKS - 1):
        for steps in range(4):
            block = pieces[piece, 16 * steps : 16 * steps + 16, :half].astype(f32)
            at = ((place[0] + 4 - steps) % 4) * half
            columns = pl.ds(pl.multiple_of(at, 128), half)
            gate[8 * piece : 8 * piece + 8, columns] = block[:8]
            up[8 * piece : 8 * piece + 8, columns] = block[8:]
        for part in range(3):
            start = 24 * piece + 8 * part
            if start < down.shape[0]:
                block = pieces[piece, 64 + 16 * part : 80 + 16 * part, :half].astype(f32)
                down[start : start + 8, :half] = block[:8]
                down[start : start + 8, half:] = block[8:, : width - half]
        block = side[piece, 128:160, :].astype(f32)
        for part in range(4):
            at = 256 * part
            stop = min(at + 256, width)
            out[8 * piece : 8 * piece + 8, at:stop] = block[8 * part : 8 * part + 8, : stop - at]

    def head(index, part):
        at = part * HEAD_DIM
        return side[index, :, at : at + HEAD_DIM].astype(f32)[:rows]

    for index in range(0, HEADS - 1, 2):
        at = index * HEAD_DIM
        query[:, at : at + 128] = jnp.concatenate([head(index, 0), head(index + 1, 0)], 1)
    query[:, (HEADS - 1) * HEAD_DIM :] = head(HEADS - 1, 0)
    both = []
    for target, part in ((key, 1), (value, 2)):
        groups = [
            head(GROUP * k, part) + head(GROUP * k + 1, part) + head(GROUP * k + 2, part)
            for k in range(KV_HEADS)
        ]
        both.append(jnp.concatenate(groups, 1))
        target[...] = both[-1].T

    def row_sums(weights, grads):
        return jnp.sum(weights[...].astype(f32) * grads[...], axis=1, keepdims=True)

    attn_sum = row_sums(w_query, query) + row_sums(w_key, both[0]) + row_sums(w_value, both[1])
    mlp_sum = row_sums(w_gate, gate) + row_sums(w_up, up)
    columns = jnp.concatenate([attn_sum, mlp_sum], 1) / gains[...]
    columns = jnp.concatenate([columns, jnp.zeros((rows, BLOCK - 2), f32)], 1)
    gain_grads[...] = columns.T[:8]


def unpack(place, pieces, side, weights, gains, units):
    vmem = pl.BlockSpec(memory_space=pltpu.VMEM)
    w_query, w_key, w_value, w_gate, w_up = weights
    rows, width = w_query.shape
    shapes = [(rows, width), (w_key.shape[1], rows), (w_value.shape[1], rows), (rows, width)]
    shapes += [w_gate.shape, w_up.shape, (units, width), (8, rows)]
    return pl.pallas_call(
        unpack_kernel,
        out_shape=tuple(jax.ShapeDtypeStruct(shape, f32) for shape in shapes),
        in_specs=whole(8),
        out_specs=(vmem,) * 8,
        compiler_params=pltpu.CompilerParams(vmem_limit_bytes=VMEM_LIMIT),
        name="unpack",
    )(place, pieces, side, *weights, gains)


def feed_forward_grads(place, hidden, grad_both, middle, dy):
    vmem = pl.BlockSpec(memory_space=pltpu.VMEM)
    span = grad_both.shape[1]
    return pl.pallas_call(
        grads_kernel,
        out_shape=(jax.ShapeDtypeStruct((4, 4, 7 * 16, span // 2), bf16),) * 2,
        in_specs=whole(4),
        out_specs=(vmem, vmem),
        scratch_shapes=[
            pltpu.VMEM((hidden.shape[1] + 8, span), f32),
            pltpu.VMEM((middle.shape[1] + 64, span), f32),
        ],
        compiler_params=pltpu.CompilerParams(vmem_limit_bytes=VMEM_LIMIT),
        name="feed_forward_grads",
    )(place, hidden, grad_both, middle, dy)


def whole(count):
    return [pl.BlockSpec(memory_space=pltpu.SMEM)] + [pl.BlockSpec(memory_space=pltpu.VMEM)] * count


def attend(order, qkv, places):
    vmem = pl.BlockSpec(memory_space=pltpu.VMEM)
    return pl.pallas_call(
        forward_kernel,
        out_shape=(
            jax.ShapeDtypeStruct((BLOCKS, HEAD_DIM, BLOCK), bf16),
            jax.ShapeDtypeStruct((BLOCKS // 2, HEAD_DIM, PAIR), f32),
            jax.ShapeDtypeStruct((BLOCKS // 2, 1, PAIR), f32),
        ),
        in_specs=whole(2),
        out_specs=(vmem, vmem, vmem),
        scratch_shapes=[
            pltpu.VMEM((LENGTH, HEAD_DIM), bf16),
            pltpu.VMEM((HEAD_DIM, LENGTH), bf16),
            pltpu.VMEM((BLOCKS // 2, HEAD_DIM, PAIR), bf16),
            pltpu.VMEM((LENGTH, BLOCK), f32),
            pltpu.VMEM((BLOCKS // 2, 1, PAIR), f32),
        ],
        compiler_params=pltpu.CompilerParams(vmem_limit_bytes=VMEM_LIMIT),
        name="attend",
    )(order, qkv, places)


def attend_back(order, qkv, places, grad_attn, attn_full, log_total, cos, sin):
    return pl.pallas_call(
        backward_kernel,
        out_shape=jax.ShapeDtypeStruct((BLOCKS, 3 * HEAD_DIM, BLOCK), bf16),
        in_specs=whole(7),
        out_specs=pl.BlockSpec(memory_space=pltpu.VMEM),
        scratch_shapes=[
            pltpu.VMEM((LENGTH, HEAD_DIM), bf16),
            pltpu.VMEM((HEAD_DIM, LENGTH), bf16),
            pltpu.VMEM((LENGTH, HEAD_DIM), bf16),
            pltpu.VMEM((BLOCKS // 2, HEAD_DIM, PAIR), bf16),
            pltpu.VMEM((BLOCKS // 2, PAIR, HEAD_DIM), bf16),
            pltpu.VMEM((BLOCKS // 2, HEAD_DIM, PAIR), bf16),
            pltpu.VMEM((BLOCKS // 2, PAIR, HEAD_DIM), bf16),
            pltpu.VMEM((LENGTH, BLOCK), f32),
            pltpu.VMEM((BLOCKS // 2, 1, PAIR), f32),
            pltpu.VMEM((LENGTH, HEAD_DIM), f32),
            pltpu.VMEM((LENGTH, HEAD_DIM), f32),
        ],
        compiler_params=pltpu.CompilerParams(vmem_limit_bytes=VMEM_LIMIT),
        name="attend_back",
    )(order, qkv, places, grad_attn, attn_full, log_total, cos, sin)


def body(
    inputs,
    positions,
    attn_gain,
    w_query,
    w_key,
    w_value,
    w_out,
    mlp_gain,
    w_gate,
    w_up,
    w_down,
    cotangent,
):
    rows, width = inputs.shape
    shard = w_query.shape[0]
    hidden = w_gate.shape[1] // lax.axis_size("x")
    chips = lax.axis_size("x")

    chip = lax.axis_index("x")
    place = jnp.stack([chip] + [lax.axis_index(k) for k in ("core", *CTX)]).astype(jnp.int32)

    spare = jnp.zeros((1, SPARE), bf16)
    gain_row = jnp.concatenate(
        [attn_gain[None, :], spare, mlp_gain[None, :], jnp.zeros((1, PACKED - 2 * BLOCK + SPARE), bf16)],
        1,
    )
    packed = jnp.concatenate(
        [
            jnp.concatenate([w_query, w_key, w_value, jnp.zeros((shard, PACKED - QKV), bf16)], 1),
            gain_row,
            jnp.zeros((SPARE - 1, PACKED), bf16),
        ],
        0,
    )
    own_w = spread(packed, "x")
    gate_up = jnp.concatenate(
        [
            jnp.swapaxes(w_gate.reshape(shard, chips, hidden), 0, 1),
            jnp.swapaxes(w_up.reshape(shard, chips, hidden), 0, 1),
        ],
        2,
    )
    own_w, gate_up = lax.optimization_barrier((own_w, gate_up))
    other_w = other_core(own_w)
    gain_rows = core_order(own_w[:, None, shard, :], other_w[:, None, shard, :], 1)
    gain_rows = gain_rows.reshape(2 * chips, PACKED).astype(f32)
    gain_one = gain_rows[:, :shard].reshape(1, width)
    gain_two = gain_rows[:, BLOCK : BLOCK + shard].reshape(1, width)
    own_w = own_w.reshape(chips * BLOCK, PACKED)
    other_w = other_w.reshape(chips * BLOCK, PACKED)

    freq = ROPE_BASE ** (-2.0 * jnp.arange(HALF).astype(f32) / HEAD_DIM)
    turn = positions.astype(f32)[None, :] * freq[:, None]
    cos, sin = jnp.cos(turn), jnp.sin(turn)

    resid = inputs.astype(f32)
    root_one = lax.rsqrt(jnp.mean(resid * resid, axis=-1, keepdims=True) + NORM_EPS)
    normed_one = resid * root_one
    hidden_one = (normed_one * gain_one).astype(bf16)

    columns = hidden_one.T.reshape(chips, 2, shard, rows)
    columns = jnp.pad(columns, ((0, 0), (0, 0), (0, SPARE), (0, 0)))
    own_columns, other_columns = core_halves(columns, 1)
    lin = dot(own_w, own_columns.reshape(chips * BLOCK, rows), 0, 0) + dot(
        other_w, other_columns.reshape(chips * BLOCK, rows), 0, 0
    )

    def rotated(part, heads):
        part = part.reshape(heads, 2, HALF, rows)
        first, second = rotate_rows(part[:, 0], part[:, 1], cos, sin)
        return jnp.concatenate([first, second], 1)

    query = (rotated(lin[:Q_WIDTH], HEADS).astype(bf16).astype(f32) * SCALE).astype(bf16)
    keys = rotated(lin[Q_WIDTH : Q_WIDTH + KV_WIDTH], KV_HEADS).astype(bf16)
    values = lin[Q_WIDTH + KV_WIDTH : QKV].astype(bf16).reshape(KV_HEADS, HEAD_DIM, rows)
    chunks = jnp.concatenate(
        [query, jnp.repeat(keys, GROUP, axis=0), jnp.repeat(values, GROUP, axis=0)], 1
    )
    chunks = jnp.concatenate([chunks, jnp.zeros((1, 3 * HEAD_DIM, rows), bf16)], 0)
    place_rows = jnp.stack([positions // BLOCK, positions % BLOCK]).astype(bf16)
    place_rows = jnp.pad(place_rows, ((0, 14), (0, 0)))
    chunks = jnp.concatenate(
        [chunks, jnp.broadcast_to(place_rows, (BLOCKS, 16, rows))], 1
    )
    qkv = exchange(chunks, CTX)
    rank = qkv[:, 3 * HEAD_DIM, 0].astype(jnp.int32)
    order = jnp.sum(
        jnp.where(
            rank[None, :] == jnp.arange(BLOCKS)[:, None], jnp.arange(BLOCKS)[None, :], 0
        ),
        axis=1,
    ).astype(jnp.int32)
    places = qkv[:, 192:193].astype(f32) * float(BLOCK) + qkv[:, 193:194].astype(f32)

    w_out, _ = lax.optimization_barrier((w_out, own_w))
    out_w = lax.all_gather(w_out, DP, axis=0, tiled=True)
    w_down_late, dy, gate_up, _ = lax.optimization_barrier((w_down, cotangent, gate_up, qkv))
    gate_up = exchange(gate_up, "x")
    turns = places * freq[None, :, None]
    cos_all, sin_all = jnp.cos(turns), jnp.sin(turns)

    attn, attn_full, log_total = attend(order, qkv, places)
    attn, gate_up = lax.optimization_barrier((attn, gate_up))
    gate_up = core_order(gate_up[:, None], other_core(gate_up)[:, None], 1)
    gate_up = gate_up.reshape(width, 2 * hidden)
    down_w = core_order(w_down_late, other_core(w_down_late), 0)
    dy = jnp.concatenate(from_chips(dy), 0)
    attn_t = exchange(attn, CTX)
    attn_t, cos_all, sin_all = lax.optimization_barrier((attn_t, cos_all, sin_all))
    attn_t = attn_t[:HEADS].reshape(Q_WIDTH, rows)

    mixed = resid + dot(attn_t, out_w, 0, 0)
    root_two = lax.rsqrt(jnp.mean(mixed * mixed, axis=-1, keepdims=True) + NORM_EPS)
    normed_two = mixed * root_two
    hidden_two = (normed_two * gain_two).astype(bf16)
    hidden_two = jnp.concatenate(from_chips(hidden_two), 0)

    early, _ = lax.optimization_barrier((hidden_one, qkv))
    seq_hidden = lax.all_gather(early, CTX, axis=0, tiled=True).reshape(BLOCKS, rows, width)

    both = dot(hidden_two, gate_up, 1, 0)
    gate, upper = both[:, :hidden], both[:, hidden:]
    sigma = jax.nn.sigmoid(gate)
    silu_gate = gate * sigma
    middle = (silu_gate * upper).astype(bf16)
    grad_middle = dot(dy, down_w, 1, 1)
    grad_both = jnp.concatenate(
        [
            (grad_middle * upper * sigma * (1.0 + gate * (1.0 - sigma))).astype(bf16),
            (grad_middle * silu_gate).astype(bf16),
        ],
        1,
    )
    grad_hidden = dot(grad_both, gate_up, 1, 1).astype(bf16)
    middle, grad_both, grad_hidden = lax.optimization_barrier((middle, grad_both, grad_hidden))
    sent = parts_of(jnp.split(grad_hidden, chips))

    keep, give = feed_forward_grads(place, hidden_two, grad_both, middle, dy)
    give, sent[1], sent[2], sent[3] = lax.optimization_barrier((give, *sent[1:]))
    pieces = (keep.astype(f32) + other_core(give).astype(f32)).astype(bf16)
    summed = lax.psum_scatter(
        pieces.reshape(-1, hidden), "ctx_1", scatter_dimension=0, tiled=True
    )
    sent[0], seq_hidden = lax.optimization_barrier((sent[0], seq_hidden))
    grad_hidden = total(jnp.stack(sent))

    grad_mixed = norm_back(normed_two, root_two, gain_two, grad_hidden, cotangent.astype(f32))
    grad_proj = grad_mixed.astype(bf16)
    grad_attn = dot(out_w, grad_proj, 1, 1).astype(bf16).reshape(HEADS, HEAD_DIM, rows)
    grad_attn = jnp.concatenate([grad_attn, jnp.zeros((1, HEAD_DIM, rows), bf16)], 0)
    grad_attn, late_proj = lax.optimization_barrier((grad_attn, grad_proj))
    grad_attn = exchange(grad_attn, CTX)

    own_attn, other_attn = core_halves(attn_t.reshape(chips, 2, shard, rows), 1)
    own_attn, other_attn = [
        dot(part.reshape(chips * shard, rows), late_proj, 1, 0) for part in (own_attn, other_attn)
    ]
    go = (own_attn + other_core(other_attn.astype(bf16)).astype(f32)).astype(bf16)
    go = summed_over(go.reshape(chips, shard, width), "x")

    grad = attend_back(order, qkv, places, grad_attn, attn_full, log_total, cos_all, sin_all)
    grad, summed = lax.optimization_barrier((grad, summed))
    pieces = lax.psum_scatter(summed, "ctx_0", scatter_dimension=0, tiled=True)
    go = jnp.pad(go, ((0, SPARE), (0, 0))).reshape(BLOCKS, 8 * width // BLOCK, BLOCK)
    go = jnp.pad(go, ((0, 0), (0, 4), (0, 0)))
    back = exchange(jnp.concatenate([grad, go], 1), CTX)
    proj_grad = lax.dot_general(
        seq_hidden, grad, (((0, 1), (0, 2)), ((), ())), preferred_element_type=f32
    )
    proj_grad = proj_grad.astype(bf16).reshape(2 * chips, shard, 3 * HEAD_DIM)
    proj_grad, back, pieces = lax.optimization_barrier((proj_grad, back, pieces))
    mine = received([pieces[16 * k : 16 * k + 16] for k in range(4)], "x")
    mine = jnp.concatenate([mine[0], mine[1], mine[3], mine[2], pieces[16 * chips :]], 0)
    mine = lax.all_gather(mine, CTX, axis=0, tiled=True).reshape(BLOCKS, -1, hidden)

    proj_grad = total(exchange(proj_grad, DP)).astype(bf16)
    proj_grad, back, late_middle = lax.optimization_barrier((proj_grad, back, middle))
    go = total(back[:, 3 * HEAD_DIM : 3 * HEAD_DIM + 8 * width // BLOCK]).astype(bf16)
    go = jnp.pad(go.reshape(8, width), ((0, 0), (0, 1024 - width)))
    side = jnp.pad(proj_grad, ((0, SPARE), (0, HEAD_DIM)))
    side = jnp.concatenate([side] + [go[:, 256 * k : 256 * k + 256] for k in range(4)], 0)
    side = spread(side, CTX)
    gains = jnp.stack([attn_gain, mlp_gain], 1).astype(f32)
    weights = (w_query, w_key, w_value, w_gate, w_up)
    query_grad, key_grad, value_grad, out_grad, gate_grad, up_grad, down_grad, gain_grads = unpack(
        place, mine, side, weights, gains, hidden // 2
    )

    out_part = jnp.split(dot(late_middle, down_w, 1, 0).astype(bf16), chips)
    output = (mixed + to_chips(out_part)).astype(bf16)
    back = back[:HEADS]
    grad_kv = total(jnp.moveaxis(back[:, HEAD_DIM : 3 * HEAD_DIM].reshape(KV_HEADS, GROUP, 2 * HEAD_DIM, rows), 1, 0))
    grad_kv = grad_kv.astype(bf16)
    grad_lin = jnp.concatenate(
        [
            back[:, :HEAD_DIM].reshape(Q_WIDTH, rows),
            grad_kv[:, :HEAD_DIM].reshape(KV_WIDTH, rows),
            grad_kv[:, HEAD_DIM:].reshape(KV_WIDTH, rows),
            jnp.zeros((PACKED - QKV, rows), bf16),
        ],
        0,
    )
    own_grad = dot(own_w, grad_lin, 1, 0).reshape(chips, 1, BLOCK, rows)[:, :, :shard]
    other_grad = dot(other_w, grad_lin, 1, 0).reshape(chips, 1, BLOCK, rows)[:, :, :shard]
    grad_hidden_one = core_order(own_grad, other_grad, 1).reshape(width, rows).T
    input_grad = norm_back(normed_one, root_one, gain_one, grad_hidden_one, grad_mixed)

    return (
        output,
        input_grad,
        gain_grads[0],
        query_grad,
        key_grad.T,
        value_grad.T,
        out_grad,
        gain_grads[1],
        gate_grad,
        up_grad,
        down_grad,
    )


def solution(mesh):
    torus = Mesh(mesh.devices.reshape(4, 2, 4, 4), ALL)
    placed = (
        P(ALL, None),
        P(ALL),
        P(DP),
        P(DP, None),
        P(DP, None),
        P(DP, None),
        P(DP, None),
        P(DP),
        P(DP, None),
        P(DP, None),
        P(DP, None),
        P(ALL, None),
    )
    return jax.shard_map(
        body,
        mesh=torus,
        in_specs=placed,
        out_specs=(
            P(ALL, None),
            P(ALL, None),
            P(DP),
            P(DP, None),
            P(DP, None),
            P(DP, None),
            P(DP, None),
            P(DP),
            P(DP, None),
            P(DP, None),
            P(DP, None),
        ),
        check_vma=False,
    )
```

```python
import jax
import jax.numpy as jnp
from jax import lax
from jax.experimental import pallas as pl
from jax.experimental.pallas import tpu as pltpu
from jax.sharding import Mesh
from jax.sharding import PartitionSpec as P

HEADS = 15
KV_HEADS = 5
GROUP = HEADS // KV_HEADS
HEAD_DIM = 64
HALF = HEAD_DIM // 2
Q_WIDTH = HEADS * HEAD_DIM
KV_WIDTH = KV_HEADS * HEAD_DIM
QKV = Q_WIDTH + 2 * KV_WIDTH
SCALE = HEAD_DIM**-0.5
ROPE_BASE = 100000.0
NORM_EPS = 1e-05
BLOCK = 128
BLOCKS = 16
PAIR = 2 * BLOCK
LENGTH = BLOCK * BLOCKS
PACKED = 1664
SPARE = 8
CHUNK = 3 * HEAD_DIM + 16

DP = ("x", "core")
CTX = ("ctx_0", "ctx_1")
ALL = DP + CTX

f32 = jnp.float32
bf16 = jnp.bfloat16
VMEM_LIMIT = 56 * 1024 * 1024


def exchange(chunks, axis):
    return lax.all_to_all(chunks, axis, split_axis=0, concat_axis=0, tiled=True)


def spread(shard, axis):
    return exchange(jnp.broadcast_to(shard, (lax.axis_size(axis), *shard.shape)), axis)


def other_core(value):
    return lax.ppermute(value, "core", [(0, 1), (1, 0)])


def shift(value, steps, axis="x"):
    return lax.ppermute(value, axis, [(k, (k + steps) % 4) for k in range(4)])


def received(parts, axis):
    return [parts[0]] + [shift(parts[k], k, axis) for k in (1, 3, 2)]


def from_chips(value):
    return [value, shift(value, 1), shift(value, 3), shift(value, 2)]


def parts_of(parts):
    return [parts[0], shift(parts[1], 3), shift(parts[2], 1), shift(parts[3], 2)]


def to_chips(parts):
    sent = parts_of(parts)
    return sent[0].astype(f32) + sent[1].astype(f32) + sent[2].astype(f32) + sent[3].astype(f32)


def exchange_chips(chunks, chip):
    result = jnp.zeros_like(chunks)
    for steps in range(4):
        part = lax.dynamic_index_in_dim(chunks, (chip + steps) % 4, 0)
        if steps:
            part = shift(part, steps)
        result = lax.dynamic_update_slice_in_dim(result, part, (chip + 4 - steps) % 4, 0)
    return result


def summed_over(chunks, axis):
    me = lax.axis_index(axis)
    parts = [
        lax.dynamic_index_in_dim(chunks, (me + k) % 4, 0, keepdims=False) for k in range(4)
    ]
    return sum(part.astype(f32) for part in received(parts, axis)).astype(bf16)


def core_order(own, other, axis):
    first = lax.axis_index("core") == 0
    return jnp.where(
        first,
        jnp.concatenate([own, other], axis),
        jnp.concatenate([other, own], axis),
    )


def core_halves(value, axis):
    core = lax.axis_index("core")
    keep = lax.dynamic_index_in_dim(value, core, axis, keepdims=False)
    give = lax.dynamic_index_in_dim(value, 1 - core, axis, keepdims=False)
    return keep, give


def core_summed(value, axis):
    keep, give = core_halves(value, axis)
    return (keep + other_core(give.astype(bf16)).astype(f32)).astype(bf16)


def total(parts):
    return jnp.sum(parts.astype(f32), axis=0)


def dot(left, right, left_dim, right_dim):
    return lax.dot_general(
        left, right, (((left_dim,), (right_dim,)), ((), ())), preferred_element_type=f32
    )


def rotate_rows(first, second, cos, sin):
    return first * cos - second * sin, second * cos + first * sin


def norm_back(normed, root, gain, grad_normed, grad_out):
    weighted = gain * grad_normed
    return (
        grad_out
        + root * weighted
        - normed * root * jnp.mean(normed * weighted, axis=-1, keepdims=True)
    )


def flip(block):
    return block.astype(f32).T.astype(bf16)


def scores_of(keys, query, key_places, query_places, span):
    scores = jnp.dot(keys, query, preferred_element_type=f32)
    places = key_places[span - 512 : span, :]
    visible = jnp.concatenate([places, places], 1) <= query_places
    tail = jnp.where(visible, scores[span - 512 :], -1e30)
    if span == 512:
        return tail
    return jnp.concatenate([scores[: span - 512], tail], 0)


def sort_places(block, rank, places, key_places, query_places):
    row = places[block]
    query_places[rank // 2, :, (rank % 2) * BLOCK : (rank % 2 + 1) * BLOCK] = row
    key_places[rank * BLOCK : (rank + 1) * BLOCK, :] = jnp.broadcast_to(row, (BLOCK, BLOCK)).T


def forward_kernel(
    order, qkv, places, attn, attn_full, log_total, keys, values, query, key_places, query_places
):
    for rank in range(BLOCKS):
        block = order[rank]
        rows = slice(rank * BLOCK, (rank + 1) * BLOCK)
        side = slice((rank % 2) * BLOCK, (rank % 2 + 1) * BLOCK)
        query[rank // 2, :, side] = qkv[block, 0:64, :]
        keys[rows, :] = flip(qkv[block, 64:128, :])
        values[:, rows] = qkv[block, 128:192, :]
        sort_places(block, rank, places, key_places, query_places)
    for quarter in range(4):
        span = 512 * (quarter + 1)

        def pair_step(step, carry, quarter=quarter, span=span):
            pair = 2 * quarter + step
            scores = scores_of(keys[:span, :], query[pair], key_places, query_places[pair], span)
            best = jnp.max(scores, axis=0, keepdims=True)
            weights = jnp.exp(scores - best)
            sums = jnp.sum(weights, axis=0, keepdims=True)
            result = jnp.dot(values[:, :span], weights.astype(bf16), preferred_element_type=f32)
            result = result / sums
            attn_full[pair] = result
            log_total[pair] = best + jnp.log(sums)
            low = result.astype(bf16)
            attn[order[2 * pair]] = low[:, :BLOCK]
            attn[order[2 * pair + 1]] = low[:, BLOCK:]
            return carry

        lax.fori_loop(0, 2, pair_step, 0, unroll=True)


def backward_kernel(
    order,
    qkv,
    places,
    grad_attn,
    attn_full,
    log_total,
    cos,
    sin,
    grad,
    keys,
    keys_wide,
    values,
    query,
    query_tall,
    out_wide,
    out_tall,
    key_places,
    query_places,
    grad_keys,
    grad_values,
):
    for rank in range(BLOCKS):
        block = order[rank]
        rows = slice(rank * BLOCK, (rank + 1) * BLOCK)
        side = slice((rank % 2) * BLOCK, (rank % 2 + 1) * BLOCK)
        query[rank // 2, :, side] = qkv[block, 0:64, :]
        query_tall[rank // 2, side, :] = flip(qkv[block, 0:64, :])
        keys_wide[:, rows] = qkv[block, 64:128, :]
        keys[rows, :] = flip(qkv[block, 64:128, :])
        values[rows, :] = flip(qkv[block, 128:192, :])
        out_wide[rank // 2, :, side] = grad_attn[block]
        out_tall[rank // 2, side, :] = flip(grad_attn[block])
        sort_places(block, rank, places, key_places, query_places)
    grad_keys[...] = jnp.zeros_like(grad_keys)
    grad_values[...] = jnp.zeros_like(grad_values)
    for quarter in range(4):
        span = 512 * (quarter + 1)

        def pair_step(step, carry, quarter=quarter, span=span):
            pair = 2 * quarter + step
            scores = scores_of(keys[:span, :], query[pair], key_places, query_places[pair], span)
            probs = jnp.exp(scores - log_total[pair])
            grad_probs = jnp.dot(values[:span, :], out_wide[pair], preferred_element_type=f32)
            delta = jnp.sum(out_wide[pair].astype(f32) * attn_full[pair], axis=0, keepdims=True)
            grad_scores = (probs * (grad_probs - delta)).astype(bf16)
            grad_query = SCALE * jnp.dot(
                keys_wide[:, :span], grad_scores, preferred_element_type=f32
            )
            grad_keys[:span, :] += jnp.dot(
                grad_scores, query_tall[pair], preferred_element_type=f32
            )
            grad_values[:span, :] += jnp.dot(
                probs.astype(bf16), out_tall[pair], preferred_element_type=f32
            )
            for part in range(2):
                block = order[2 * pair + part]
                piece = grad_query[:, part * BLOCK : (part + 1) * BLOCK]
                first, second = rotate_rows(piece[:HALF], piece[HALF:], cos[block], -sin[block])
                grad[block, 0:32, :] = first.astype(bf16)
                grad[block, 32:64, :] = second.astype(bf16)
            return carry

        lax.fori_loop(0, 2, pair_step, 0, unroll=True)
    for rank in range(BLOCKS):
        block = order[rank]
        rows = slice(rank * BLOCK, (rank + 1) * BLOCK)
        piece = grad_keys[rows, :].T
        first, second = rotate_rows(piece[:HALF], piece[HALF:], cos[block], -sin[block])
        grad[block, 64:96, :] = first.astype(bf16)
        grad[block, 96:128, :] = second.astype(bf16)
        grad[block, 128:192, :] = grad_values[rows, :].T.astype(bf16)


def grads_kernel(place, hidden, grad_both, middle, dy, keep, give, wide, tall):
    width, span = hidden.shape[1], grad_both.shape[1]
    units = middle.shape[1]
    wide[0:width, :] = lax.dot_general(
        hidden[...], grad_both[...], (((0,), (0,)), ((), ())), preferred_element_type=f32
    )
    wide[width : width + 8, :] = jnp.zeros((8, span), f32)
    tall[...] = jnp.zeros_like(tall)
    tall[0:units, 0:width] = lax.dot_general(
        middle[...], dy[...], (((0,), (0,)), ((), ())), preferred_element_type=f32
    )
    shard = width // 8
    half = span // 2
    for target, side in ((keep, place[1]), (give, 1 - place[1])):

        def step(piece, carry, target=target, side=side):
            first, second = piece // 4, piece % 4
            for part in range(7):
                if part < 4:
                    start = (2 * part + side) * shard + 8 * piece
                    block = wide[pl.ds(pl.multiple_of(start, 8), 8), :]
                    slot = (part + 4 - place[0]) % 4
                else:
                    start = side * (units // 2) + 24 * piece + 8 * (part - 4)
                    block = tall[pl.ds(pl.multiple_of(start, 8), 8), :]
                    slot = part
                target[second, first, pl.ds(pl.multiple_of(16 * slot, 16), 16), :] = (
                    jnp.concatenate([block[:, :half], block[:, half:]], 0).astype(bf16)
                )
            return carry

        lax.fori_loop(0, BLOCKS, step, 0)


def unpack_kernel(
    place,
    pieces,
    side,
    w_query,
    w_key,
    w_value,
    w_gate,
    w_up,
    gains,
    query,
    key,
    value,
    out,
    gate,
    up,
    down,
    gain_grads,
):
    half = gate.shape[1] // 4
    rows = query.shape[0]
    width = down.shape[1]
    for piece in range(BLOCKS - 1):
        for steps in range(4):
            block = pieces[piece, 16 * steps : 16 * steps + 16, :half].astype(f32)
            at = ((place[0] + 4 - steps) % 4) * half
            columns = pl.ds(pl.multiple_of(at, 128), half)
            gate[8 * piece : 8 * piece + 8, columns] = block[:8]
            up[8 * piece : 8 * piece + 8, columns] = block[8:]
        for part in range(3):
            start = 24 * piece + 8 * part
            if start < down.shape[0]:
                block = pieces[piece, 64 + 16 * part : 80 + 16 * part, :half].astype(f32)
                down[start : start + 8, :half] = block[:8]
                down[start : start + 8, half:] = block[8:, : width - half]
        block = side[piece, 128:160, :].astype(f32)
        for part in range(4):
            at = 256 * part
            stop = min(at + 256, width)
            out[8 * piece : 8 * piece + 8, at:stop] = block[8 * part : 8 * part + 8, : stop - at]

    def head(index, part):
        at = part * HEAD_DIM
        return side[index, :, at : at + HEAD_DIM].astype(f32)[:rows]

    for index in range(0, HEADS - 1, 2):
        at = index * HEAD_DIM
        query[:, at : at + 128] = jnp.concatenate([head(index, 0), head(index + 1, 0)], 1)
    query[:, (HEADS - 1) * HEAD_DIM :] = head(HEADS - 1, 0)
    both = []
    for target, part in ((key, 1), (value, 2)):
        groups = [
            head(GROUP * k, part) + head(GROUP * k + 1, part) + head(GROUP * k + 2, part)
            for k in range(KV_HEADS)
        ]
        both.append(jnp.concatenate(groups, 1))
        target[...] = both[-1].T

    def row_sums(weights, grads):
        return jnp.sum(weights[...].astype(f32) * grads[...], axis=1, keepdims=True)

    attn_sum = row_sums(w_query, query) + row_sums(w_key, both[0]) + row_sums(w_value, both[1])
    mlp_sum = row_sums(w_gate, gate) + row_sums(w_up, up)
    columns = jnp.concatenate([attn_sum, mlp_sum], 1) / gains[...]
    columns = jnp.concatenate([columns, jnp.zeros((rows, BLOCK - 2), f32)], 1)
    gain_grads[...] = columns.T[:8]


def unpack(place, pieces, side, weights, gains, units):
    vmem = pl.BlockSpec(memory_space=pltpu.VMEM)
    w_query, w_key, w_value, w_gate, w_up = weights
    rows, width = w_query.shape
    shapes = [(rows, width), (w_key.shape[1], rows), (w_value.shape[1], rows), (rows, width)]
    shapes += [w_gate.shape, w_up.shape, (units, width), (8, rows)]
    return pl.pallas_call(
        unpack_kernel,
        out_shape=tuple(jax.ShapeDtypeStruct(shape, f32) for shape in shapes),
        in_specs=whole(8),
        out_specs=(vmem,) * 8,
        compiler_params=pltpu.CompilerParams(vmem_limit_bytes=VMEM_LIMIT),
        name="unpack",
    )(place, pieces, side, *weights, gains)


def feed_forward_grads(place, hidden, grad_both, middle, dy):
    vmem = pl.BlockSpec(memory_space=pltpu.VMEM)
    span = grad_both.shape[1]
    return pl.pallas_call(
        grads_kernel,
        out_shape=(jax.ShapeDtypeStruct((4, 4, 7 * 16, span // 2), bf16),) * 2,
        in_specs=whole(4),
        out_specs=(vmem, vmem),
        scratch_shapes=[
            pltpu.VMEM((hidden.shape[1] + 8, span), f32),
            pltpu.VMEM((middle.shape[1] + 64, span), f32),
        ],
        compiler_params=pltpu.CompilerParams(vmem_limit_bytes=VMEM_LIMIT),
        name="feed_forward_grads",
    )(place, hidden, grad_both, middle, dy)


def whole(count):
    return [pl.BlockSpec(memory_space=pltpu.SMEM)] + [pl.BlockSpec(memory_space=pltpu.VMEM)] * count


def attend(order, qkv, places):
    vmem = pl.BlockSpec(memory_space=pltpu.VMEM)
    return pl.pallas_call(
        forward_kernel,
        out_shape=(
            jax.ShapeDtypeStruct((BLOCKS, HEAD_DIM, BLOCK), bf16),
            jax.ShapeDtypeStruct((BLOCKS // 2, HEAD_DIM, PAIR), f32),
            jax.ShapeDtypeStruct((BLOCKS // 2, 1, PAIR), f32),
        ),
        in_specs=whole(2),
        out_specs=(vmem, vmem, vmem),
        scratch_shapes=[
            pltpu.VMEM((LENGTH, HEAD_DIM), bf16),
            pltpu.VMEM((HEAD_DIM, LENGTH), bf16),
            pltpu.VMEM((BLOCKS // 2, HEAD_DIM, PAIR), bf16),
            pltpu.VMEM((LENGTH, BLOCK), f32),
            pltpu.VMEM((BLOCKS // 2, 1, PAIR), f32),
        ],
        compiler_params=pltpu.CompilerParams(vmem_limit_bytes=VMEM_LIMIT),
        name="attend",
    )(order, qkv, places)


def attend_back(order, qkv, places, grad_attn, attn_full, log_total, cos, sin):
    return pl.pallas_call(
        backward_kernel,
        out_shape=jax.ShapeDtypeStruct((BLOCKS, 3 * HEAD_DIM, BLOCK), bf16),
        in_specs=whole(7),
        out_specs=pl.BlockSpec(memory_space=pltpu.VMEM),
        scratch_shapes=[
            pltpu.VMEM((LENGTH, HEAD_DIM), bf16),
            pltpu.VMEM((HEAD_DIM, LENGTH), bf16),
            pltpu.VMEM((LENGTH, HEAD_DIM), bf16),
            pltpu.VMEM((BLOCKS // 2, HEAD_DIM, PAIR), bf16),
            pltpu.VMEM((BLOCKS // 2, PAIR, HEAD_DIM), bf16),
            pltpu.VMEM((BLOCKS // 2, HEAD_DIM, PAIR), bf16),
            pltpu.VMEM((BLOCKS // 2, PAIR, HEAD_DIM), bf16),
            pltpu.VMEM((LENGTH, BLOCK), f32),
            pltpu.VMEM((BLOCKS // 2, 1, PAIR), f32),
            pltpu.VMEM((LENGTH, HEAD_DIM), f32),
            pltpu.VMEM((LENGTH, HEAD_DIM), f32),
        ],
        compiler_params=pltpu.CompilerParams(vmem_limit_bytes=VMEM_LIMIT),
        name="attend_back",
    )(order, qkv, places, grad_attn, attn_full, log_total, cos, sin)


def body(
    inputs,
    positions,
    attn_gain,
    w_query,
    w_key,
    w_value,
    w_out,
    mlp_gain,
    w_gate,
    w_up,
    w_down,
    cotangent,
):
    rows, width = inputs.shape
    shard = w_query.shape[0]
    hidden = w_gate.shape[1] // lax.axis_size("x")
    chips = lax.axis_size("x")

    chip = lax.axis_index("x")
    place = jnp.stack([chip] + [lax.axis_index(k) for k in ("core", *CTX)]).astype(jnp.int32)

    spare = jnp.zeros((1, SPARE), bf16)
    gain_row = jnp.concatenate(
        [attn_gain[None, :], spare, mlp_gain[None, :], jnp.zeros((1, PACKED - 2 * BLOCK + SPARE), bf16)],
        1,
    )
    packed = jnp.concatenate(
        [
            jnp.concatenate([w_query, w_key, w_value, jnp.zeros((shard, PACKED - QKV), bf16)], 1),
            gain_row,
            jnp.zeros((SPARE - 1, PACKED), bf16),
        ],
        0,
    )
    own_w = spread(packed, "x")
    gate_up = jnp.concatenate(
        [
            jnp.swapaxes(w_gate.reshape(shard, chips, hidden), 0, 1),
            jnp.swapaxes(w_up.reshape(shard, chips, hidden), 0, 1),
        ],
        2,
    )
    own_w, gate_up = lax.optimization_barrier((own_w, gate_up))
    other_w = other_core(own_w)
    gain_rows = core_order(own_w[:, None, shard, :], other_w[:, None, shard, :], 1)
    gain_rows = gain_rows.reshape(2 * chips, PACKED).astype(f32)
    gain_one = gain_rows[:, :shard].reshape(1, width)
    gain_two = gain_rows[:, BLOCK : BLOCK + shard].reshape(1, width)
    own_w = own_w.reshape(chips * BLOCK, PACKED)
    other_w = other_w.reshape(chips * BLOCK, PACKED)

    freq = ROPE_BASE ** (-2.0 * jnp.arange(HALF).astype(f32) / HEAD_DIM)
    turn = positions.astype(f32)[None, :] * freq[:, None]
    cos, sin = jnp.cos(turn), jnp.sin(turn)

    resid = inputs.astype(f32)
    root_one = lax.rsqrt(jnp.mean(resid * resid, axis=-1, keepdims=True) + NORM_EPS)
    normed_one = resid * root_one
    hidden_one = (normed_one * gain_one).astype(bf16)

    columns = hidden_one.T.reshape(chips, 2, shard, rows)
    columns = jnp.pad(columns, ((0, 0), (0, 0), (0, SPARE), (0, 0)))
    own_columns, other_columns = core_halves(columns, 1)
    lin = dot(own_w, own_columns.reshape(chips * BLOCK, rows), 0, 0) + dot(
        other_w, other_columns.reshape(chips * BLOCK, rows), 0, 0
    )

    def rotated(part, heads):
        part = part.reshape(heads, 2, HALF, rows)
        first, second = rotate_rows(part[:, 0], part[:, 1], cos, sin)
        return jnp.concatenate([first, second], 1)

    query = (rotated(lin[:Q_WIDTH], HEADS).astype(bf16).astype(f32) * SCALE).astype(bf16)
    keys = rotated(lin[Q_WIDTH : Q_WIDTH + KV_WIDTH], KV_HEADS).astype(bf16)
    values = lin[Q_WIDTH + KV_WIDTH : QKV].astype(bf16).reshape(KV_HEADS, HEAD_DIM, rows)
    chunks = jnp.concatenate(
        [query, jnp.repeat(keys, GROUP, axis=0), jnp.repeat(values, GROUP, axis=0)], 1
    )
    chunks = jnp.concatenate([chunks, jnp.zeros((1, 3 * HEAD_DIM, rows), bf16)], 0)
    place_rows = jnp.stack([positions // BLOCK, positions % BLOCK]).astype(bf16)
    place_rows = jnp.pad(place_rows, ((0, 14), (0, 0)))
    chunks = jnp.concatenate(
        [chunks, jnp.broadcast_to(place_rows, (BLOCKS, 16, rows))], 1
    )
    qkv = exchange(chunks, CTX)
    rank = qkv[:, 3 * HEAD_DIM, 0].astype(jnp.int32)
    order = jnp.sum(
        jnp.where(
            rank[None, :] == jnp.arange(BLOCKS)[:, None], jnp.arange(BLOCKS)[None, :], 0
        ),
        axis=1,
    ).astype(jnp.int32)
    places = qkv[:, 192:193].astype(f32) * float(BLOCK) + qkv[:, 193:194].astype(f32)

    w_out, _ = lax.optimization_barrier((w_out, own_w))
    out_w = lax.all_gather(w_out, DP, axis=0, tiled=True)
    w_down_late, dy, gate_up, _ = lax.optimization_barrier((w_down, cotangent, gate_up, qkv))
    gate_up = exchange(gate_up, "x")
    turns = places * freq[None, :, None]
    cos_all, sin_all = jnp.cos(turns), jnp.sin(turns)

    attn, attn_full, log_total = attend(order, qkv, places)
    attn, gate_up = lax.optimization_barrier((attn, gate_up))
    gate_up = core_order(gate_up[:, None], other_core(gate_up)[:, None], 1)
    gate_up = gate_up.reshape(width, 2 * hidden)
    down_w = core_order(w_down_late, other_core(w_down_late), 0)
    dy = jnp.concatenate(from_chips(dy), 0)
    attn_t = exchange(attn, CTX)
    attn_t, cos_all, sin_all = lax.optimization_barrier((attn_t, cos_all, sin_all))
    attn_t = attn_t[:HEADS].reshape(Q_WIDTH, rows)

    mixed = resid + dot(attn_t, out_w, 0, 0)
    root_two = lax.rsqrt(jnp.mean(mixed * mixed, axis=-1, keepdims=True) + NORM_EPS)
    normed_two = mixed * root_two
    hidden_two = (normed_two * gain_two).astype(bf16)
    hidden_two = jnp.concatenate(from_chips(hidden_two), 0)

    early, _ = lax.optimization_barrier((hidden_one, qkv))
    seq_hidden = lax.all_gather(early, CTX, axis=0, tiled=True).reshape(BLOCKS, rows, width)

    both = dot(hidden_two, gate_up, 1, 0)
    gate, upper = both[:, :hidden], both[:, hidden:]
    sigma = jax.nn.sigmoid(gate)
    silu_gate = gate * sigma
    middle = (silu_gate * upper).astype(bf16)
    grad_middle = dot(dy, down_w, 1, 1)
    grad_both = jnp.concatenate(
        [
            (grad_middle * upper * sigma * (1.0 + gate * (1.0 - sigma))).astype(bf16),
            (grad_middle * silu_gate).astype(bf16),
        ],
        1,
    )
    grad_hidden = dot(grad_both, gate_up, 1, 1).astype(bf16)
    middle, grad_both, grad_hidden = lax.optimization_barrier((middle, grad_both, grad_hidden))
    sent = parts_of(jnp.split(grad_hidden, chips))

    keep, give = feed_forward_grads(place, hidden_two, grad_both, middle, dy)
    give, sent[1], sent[2], sent[3] = lax.optimization_barrier((give, *sent[1:]))
    pieces = (keep.astype(f32) + other_core(give).astype(f32)).astype(bf16)
    summed = lax.psum_scatter(
        pieces.reshape(-1, hidden), "ctx_1", scatter_dimension=0, tiled=True
    )
    sent[0], seq_hidden = lax.optimization_barrier((sent[0], seq_hidden))
    grad_hidden = total(jnp.stack(sent))

    grad_mixed = norm_back(normed_two, root_two, gain_two, grad_hidden, cotangent.astype(f32))
    grad_proj = grad_mixed.astype(bf16)
    grad_attn = dot(out_w, grad_proj, 1, 1).astype(bf16).reshape(HEADS, HEAD_DIM, rows)
    grad_attn = jnp.concatenate([grad_attn, jnp.zeros((1, HEAD_DIM, rows), bf16)], 0)
    grad_attn, late_proj = lax.optimization_barrier((grad_attn, grad_proj))
    grad_attn = exchange(grad_attn, CTX)

    own_attn, other_attn = core_halves(attn_t.reshape(chips, 2, shard, rows), 1)
    own_attn, other_attn = [
        dot(part.reshape(chips * shard, rows), late_proj, 1, 0) for part in (own_attn, other_attn)
    ]
    go = (own_attn + other_core(other_attn.astype(bf16)).astype(f32)).astype(bf16)
    go = summed_over(go.reshape(chips, shard, width), "x")

    grad = attend_back(order, qkv, places, grad_attn, attn_full, log_total, cos_all, sin_all)
    grad, summed = lax.optimization_barrier((grad, summed))
    pieces = lax.psum_scatter(summed, "ctx_0", scatter_dimension=0, tiled=True)
    go = jnp.pad(go, ((0, SPARE), (0, 0))).reshape(BLOCKS, 8 * width // BLOCK, BLOCK)
    go = jnp.pad(go, ((0, 0), (0, 4), (0, 0)))
    back = exchange(jnp.concatenate([grad, go], 1), CTX)
    proj_grad = lax.dot_general(
        seq_hidden, grad, (((0, 1), (0, 2)), ((), ())), preferred_element_type=f32
    )
    proj_grad = proj_grad.astype(bf16).reshape(2 * chips, shard, 3 * HEAD_DIM)
    proj_grad, back, pieces = lax.optimization_barrier((proj_grad, back, pieces))
    mine = received([pieces[16 * k : 16 * k + 16] for k in range(4)], "x")
    mine = jnp.concatenate([mine[0], mine[1], mine[3], mine[2], pieces[16 * chips :]], 0)
    mine = lax.all_gather(mine, CTX, axis=0, tiled=True).reshape(BLOCKS, -1, hidden)

    proj_grad = total(exchange(proj_grad, DP)).astype(bf16)
    proj_grad, back, late_middle = lax.optimization_barrier((proj_grad, back, middle))
    go = total(back[:, 3 * HEAD_DIM : 3 * HEAD_DIM + 8 * width // BLOCK]).astype(bf16)
    go = jnp.pad(go.reshape(8, width), ((0, 0), (0, 1024 - width)))
    side = jnp.pad(proj_grad, ((0, SPARE), (0, HEAD_DIM)))
    side = jnp.concatenate([side] + [go[:, 256 * k : 256 * k + 256] for k in range(4)], 0)
    side = spread(side, CTX)
    gains = jnp.stack([attn_gain, mlp_gain], 1).astype(f32)
    weights = (w_query, w_key, w_value, w_gate, w_up)
    query_grad, key_grad, value_grad, out_grad, gate_grad, up_grad, down_grad, gain_grads = unpack(
        place, mine, side, weights, gains, hidden // 2
    )

    out_part = jnp.split(dot(late_middle, down_w, 1, 0).astype(bf16), chips)
    output = (mixed + to_chips(out_part)).astype(bf16)
    back = back[:HEADS]
    grad_kv = total(jnp.moveaxis(back[:, HEAD_DIM : 3 * HEAD_DIM].reshape(KV_HEADS, GROUP, 2 * HEAD_DIM, rows), 1, 0))
    grad_kv = grad_kv.astype(bf16)
    grad_lin = jnp.concatenate(
        [
            back[:, :HEAD_DIM].reshape(Q_WIDTH, rows),
            grad_kv[:, :HEAD_DIM].reshape(KV_WIDTH, rows),
            grad_kv[:, HEAD_DIM:].reshape(KV_WIDTH, rows),
            jnp.zeros((PACKED - QKV, rows), bf16),
        ],
        0,
    )
    own_grad = dot(own_w, grad_lin, 1, 0).reshape(chips, 1, BLOCK, rows)[:, :, :shard]
    other_grad = dot(other_w, grad_lin, 1, 0).reshape(chips, 1, BLOCK, rows)[:, :, :shard]
    grad_hidden_one = core_order(own_grad, other_grad, 1).reshape(width, rows).T
    input_grad = norm_back(normed_one, root_one, gain_one, grad_hidden_one, grad_mixed)

    return (
        output,
        input_grad,
        gain_grads[0],
        query_grad,
        key_grad.T,
        value_grad.T,
        out_grad,
        gain_grads[1],
        gate_grad,
        up_grad,
        down_grad,
    )


def solution(mesh):
    torus = Mesh(mesh.devices.reshape(4, 2, 4, 4), ALL)
    placed = (
        P(ALL, None),
        P(ALL),
        P(DP),
        P(DP, None),
        P(DP, None),
        P(DP, None),
        P(DP, None),
        P(DP),
        P(DP, None),
        P(DP, None),
        P(DP, None),
        P(ALL, None),
    )
    return jax.shard_map(
        body,
        mesh=torus,
        in_specs=placed,
        out_specs=(
            P(ALL, None),
            P(ALL, None),
            P(DP),
            P(DP, None),
            P(DP, None),
            P(DP, None),
            P(DP, None),
            P(DP),
            P(DP, None),
            P(DP, None),
            P(DP, None),
        ),
        check_vma=False,
    )
```
